256 devices in a mesh: seq: 64 (over x, z_hi, y), head: 4 (over z_lo, core).
Axes of the slice: x: 4, y: 4, z: 8 (z_hi: 4, z_lo: 2; z = z_hi * 2 + z_lo), core: 2. Of those that a mesh axis runs over, the one named last changes fastest.
Arguments:
- query_act: bfloat16 [32768, 1024], P('seq', 'head'), may hold values from -24 to 24
- key_act: bfloat16 [32768, 1024], P('seq', 'head'), may hold values from -6 to 6
- value_act: bfloat16 [32768, 1024], P('seq', 'head'), may hold values from -6 to 6
- out_weight: bfloat16 [1024, 1024], P('head'), may hold values from -0.1875 to 0.1875
- cotangent: bfloat16 [32768, 1024], P('seq', 'head'), may hold values from -16 to 16
Outputs:
- mixed_out: bfloat16 [32768, 1024], P('seq', 'head')
- query_grad: bfloat16 [32768, 1024], P('seq', 'head')
- key_grad: bfloat16 [32768, 1024], P('seq', 'head')
- value_grad: bfloat16 [32768, 1024], P('seq', 'head')
- weight_grad: float32 [1024, 1024], P('head', 'seq')
The draws below stay inside these ranges and needn't reach their ends.
All inputs are finite; a program needn't handle non-finite values.
Results may differ from the reference program's by a relative error of at most 0.0065.
Values may be sent and summed in bfloat16 or wider, within the bound.
No kernel may reach another device: no remote copies, remote signals or barrier semaphores. Data moves between devices by JAX's collectives and lax.ppermute only.
A program may use at most 128 MiB of HBM per device.

```python
import jax
import jax.numpy as jnp
from jax import lax

HEADS = 16
HEAD_DIM = 64
TOK_DEV = 512
GROUP2 = 4
D = 1024
TOKENS = 32768
GROUP3 = 16
GROUP4 = 64


def draw_key_act(key, part):
    key = jax.random.fold_in(key, 11)
    result = jnp.clip(jax.random.normal(key, (TOKENS, D), jnp.float32), -6.0, 6.0)
    return result.astype(jnp.bfloat16)


def draw_query_act(key, part):
    key = jax.random.fold_in(key, 23)
    result = jnp.clip(jax.random.normal(key, (TOKENS, D), jnp.float32), -6.0, 6.0)
    return result.astype(jnp.bfloat16)


def raised(entries, stream_key, source, target, blocks, factor):
    def block_of(position):
        return (jnp.arange(entries.shape[position]) // (entries.shape[position] // blocks)).reshape((-1,) + (1,) * (entries.ndim - 1 - position))

    near = jax.random.permutation(stream_key, blocks)[block_of(target)]
    far = (block_of(target) + blocks // 2) % blocks
    return jnp.where((block_of(source) == near) | (block_of(source) == far), factor * entries, entries)


def block_levels(stream_key, shape, shards, smallest, high):
    def one(axis_at, shards_of):
        draws = jax.random.uniform(jax.random.fold_in(jax.random.fold_in(stream_key, 6), axis_at), (shards_of,), jnp.float32, smallest / len(shards), high / len(shards))
        return jnp.repeat(jnp.exp(draws), shape[axis_at] // shards_of).reshape((-1,) + (1,) * (len(shape) - axis_at - 1))

    factor_of = one(*shards[0])
    for cut in shards[1:]:
        factor_of = factor_of * one(*cut)
    return factor_of


def normal_values(own_key, dims, width, limit, split=(), kind=jnp.bfloat16):
    values = width * jax.random.normal(own_key, dims, jnp.float32)
    if split:
        values = values * block_levels(own_key, dims, split, -0.22, 0.18)
    return jnp.clip(values, -limit, limit).astype(kind)


def gaussian_with(own_key, dims, spread, limit, split, heavy, kind=jnp.bfloat16):
    array = spread * jax.random.normal(own_key, dims, jnp.float32)
    if split:
        array = array * block_levels(own_key, dims, split, -0.22, 0.18)
    return jnp.clip(raised(array, jax.random.fold_in(own_key, 3), *heavy), -limit, limit).astype(kind)


def setup_inputs(seed: int = 0) -> dict:
    key_of = jax.random.split(jax.random.key(seed), 6)
    query_act = draw_query_act(jax.random.fold_in(key_of[5], 71), 0)
    key_act = draw_key_act(jax.random.fold_in(key_of[5], 71), 0)
    value_act = normal_values(key_of[2], (TOKENS, D), 1.0, 6.0, ((0, 64), (1, 4)))
    out_weight = normal_values(key_of[3], (D, D), D ** -0.5, 0.1875, ((0, 4),))
    cotangent = gaussian_with(key_of[4], (TOKENS, D), 1.0, 16.0, ((0, 64), (1, 4)), (0, 1, 64, 4.0))
    return {"query_act": query_act, "key_act": key_act, "value_act": value_act, "out_weight": out_weight, "cotangent": cotangent}


NEG = -1e30


def select_rows(source, group_size, offset):
    return source.reshape((source.shape[0] // group_size, group_size) + source.shape[1:])[:, offset]


def spread_rows(picked, group_size, offset, filler):
    widened = jnp.full((picked.shape[0], group_size) + picked.shape[1:], filler, picked.dtype)
    widened = widened.at[:, offset].set(picked)
    return widened.reshape((picked.shape[0] * group_size,) + picked.shape[1:])


def segment_forward(pieces):
    query_rows, key_rows, value_rows = pieces
    scores = jnp.dot(query_rows, key_rows.T, preferred_element_type=jnp.float32) * (HEAD_DIM ** -0.5)
    peaks = jnp.max(scores, axis=1)
    weights = jnp.exp(scores - peaks[:, None])
    totals = jnp.sum(weights, axis=1)
    weighted = jnp.dot(weights.astype(jnp.bfloat16), value_rows, preferred_element_type=jnp.float32)
    return peaks, totals, weighted


def segment_backward(pieces):
    query_rows, key_rows, value_rows, grad_rows, log_total, delta_rows = pieces
    scores = jnp.dot(query_rows, key_rows.T, preferred_element_type=jnp.float32) * (HEAD_DIM ** -0.5)
    softmax = jnp.exp(scores - log_total[:, None])
    value_term = jnp.dot(softmax.astype(jnp.bfloat16).T, grad_rows, preferred_element_type=jnp.float32)
    prob_grad = jnp.dot(grad_rows, value_rows.T, preferred_element_type=jnp.float32)
    score_grad = (softmax * (prob_grad - delta_rows[:, None])).astype(jnp.bfloat16)
    query_term = jnp.dot(score_grad, key_rows, preferred_element_type=jnp.float32) * (HEAD_DIM ** -0.5)
    key_term = jnp.dot(score_grad.T, query_rows, preferred_element_type=jnp.float32) * (HEAD_DIM ** -0.5)
    return query_term, key_term, value_term


def reference(query_act, key_act, value_act, out_weight, cotangent):
    group_list = (1, GROUP2, GROUP3, GROUP4)
    out_heads = []
    lse_heads = []
    for head_num in range(HEADS):
        columns = slice(head_num * HEAD_DIM, (head_num + 1) * HEAD_DIM)
        sources = (query_act[:, columns], key_act[:, columns], value_act[:, columns])
        peak_list, total_list, weighted_list = [], [], []
        for group_size in group_list:
            offset = head_num % group_size
            segments = TOKENS // (group_size * TOK_DEV)
            pieces = tuple(select_rows(member, group_size, offset).reshape(segments, TOK_DEV, HEAD_DIM) for member in sources)
            peaks, totals, weighted = lax.map(segment_forward, pieces)
            peak_list.append(spread_rows(peaks.reshape(-1), group_size, offset, NEG))
            total_list.append(spread_rows(totals.reshape(-1), group_size, offset, 0.0))
            weighted_list.append(spread_rows(weighted.reshape(-1, HEAD_DIM), group_size, offset, 0.0))
        top_peak = jnp.max(jnp.stack(peak_list, 0), axis=0)
        factors = [jnp.exp(member - top_peak) for member in peak_list]
        denominator = sum(factors[level] * total_list[level] for level in range(4))
        numerator = sum(factors[level][:, None] * weighted_list[level] for level in range(4))
        out_heads.append(numerator / denominator[:, None])
        lse_heads.append(top_peak + jnp.log(denominator))
    out_full = jnp.concatenate(out_heads, 1)
    attended = out_full.astype(jnp.bfloat16)
    mixed_out = jnp.dot(attended, out_weight, preferred_element_type=jnp.float32).astype(jnp.bfloat16)
    attn_grad = jnp.dot(cotangent, out_weight.T, preferred_element_type=jnp.float32).astype(jnp.bfloat16)
    weight_grad = jnp.dot(attended.T, cotangent, preferred_element_type=jnp.float32)
    query_heads, key_heads, value_heads = [], [], []
    for head_num in range(HEADS):
        columns = slice(head_num * HEAD_DIM, (head_num + 1) * HEAD_DIM)
        grad_head = attn_grad[:, columns]
        delta_head = jnp.sum(grad_head.astype(jnp.float32) * out_full[:, columns], axis=1)
        sources = (query_act[:, columns], key_act[:, columns], value_act[:, columns], grad_head, lse_heads[head_num], delta_head)
        query_sum = jnp.zeros((TOKENS, HEAD_DIM), jnp.float32)
        key_sum = jnp.zeros((TOKENS, HEAD_DIM), jnp.float32)
        value_sum = jnp.zeros((TOKENS, HEAD_DIM), jnp.float32)
        for group_size in group_list:
            offset = head_num % group_size
            segments = TOKENS // (group_size * TOK_DEV)
            pieces = tuple(select_rows(member, group_size, offset).reshape((segments, TOK_DEV) + member.shape[1:]) for member in sources)
            query_term, key_term, value_term = lax.map(segment_backward, pieces)
            query_sum = query_sum + spread_rows(query_term.reshape(-1, HEAD_DIM), group_size, offset, 0.0)
            key_sum = key_sum + spread_rows(key_term.reshape(-1, HEAD_DIM), group_size, offset, 0.0)
            value_sum = value_sum + spread_rows(value_term.reshape(-1, HEAD_DIM), group_size, offset, 0.0)
        query_heads.append(query_sum)
        key_heads.append(key_sum)
        value_heads.append(value_sum)
    query_grad = jnp.concatenate(query_heads, 1).astype(jnp.bfloat16)
    key_grad = jnp.concatenate(key_heads, 1).astype(jnp.bfloat16)
    value_grad = jnp.concatenate(value_heads, 1).astype(jnp.bfloat16)
    return mixed_out, query_grad, key_grad, value_grad, weight_grad
```

```python
import functools

import jax
import jax.numpy as jnp
from jax import lax
from jax.experimental import pallas as pl
from jax.experimental.pallas import tpu as pltpu
from jax.sharding import PartitionSpec as P

HD = 64
NH = 4
T = 512
F = NH * HD
SEL2, SEL3, SEL4 = 128, 32, 8
SCALE = HD ** -0.5
NEG = -1e30
BF = jnp.bfloat16
F32 = jnp.float32


def iota(shape, dim):
    return lax.broadcasted_iota(jnp.int32, shape, dim)


def token_of(index):
    return (index >> 7) + ((index >> 5) & 3) * 4 + ((index >> 3) & 3) * 16 + (index & 7) * 64


def pick_mat(head, rows):
    wanted = (token_of(iota((rows, T), 0)) + head) & (T - 1)
    return jnp.where(wanted == iota((rows, T), 1), 1.0, 0.0).astype(BF)


def put_mat(head, cols):
    wanted = (token_of(iota((T, cols), 1)) + head) & (T - 1)
    return jnp.where(wanted == iota((T, cols), 0), 1.0, 0.0).astype(BF)


def dot(a, b, dims=((1,), (0,))):
    return lax.dot_general(a, b, (dims, ((), ())), preferred_element_type=F32)


def per_head_rows(mats, arrays):
    pairs = []
    for p in range(2):
        both = jnp.concatenate([a[:, 128 * p:128 * p + 128] for a in arrays], 1)
        even = dot(mats[2 * p], both)
        odd = dot(mats[2 * p + 1], both)
        pairs.append(jnp.where((iota(even.shape, 1) & 127) < HD, even, odd))
    return [
        jnp.concatenate([pair[:, 128 * n:128 * n + 128] for pair in pairs], 1)
        for n in range(len(arrays))
    ]


def head_blocks(rows, n):
    part = rows[:n]
    lane_head = iota(part.shape, 1) >> 6
    return jnp.concatenate([jnp.where(lane_head == h, part, 0.0) for h in range(NH)], 0)


def blocks_both(rows, n):
    full = head_blocks(rows, n)
    if NH * n < 128:
        full = jnp.concatenate([full, jnp.zeros((128 - NH * n, F), F32)], 0)
    return full.astype(BF), full.T.astype(BF)


def to_lanes(rows, n):
    total = None
    for h in range(NH):
        row = jnp.broadcast_to(jnp.where(iota((1, 128), 1) < n, rows[h], 0.0), (8, 128))
        if h:
            row = pltpu.roll(row, n * h, 1)
        total = row if total is None else total + row
    return total[0:1]


def from_lanes(rows, h, n, fill):
    if h:
        rows = pltpu.roll(rows, 128 - n * h, 1)
    return jnp.where(iota(rows.shape, 1) < n, rows, fill)


def soft(scores):
    peak = jnp.max(scores, axis=0, keepdims=True)
    weights = jnp.exp(scores - peak)
    return peak, jnp.sum(weights, axis=0, keepdims=True), weights.astype(BF)


def forward(keys, values, q_t):
    peak, total, weights = soft(dot(keys, q_t))
    return peak, total, dot(values, weights, ((0,), (0,)))


def backward(keys, values, q, q_t, g, g_t, lse, delta):
    prob = jnp.exp(dot(keys, q_t) - lse)
    ds = (prob * (dot(values, g_t) - delta)).astype(BF)
    d_values = dot(prob.astype(BF), g)
    d_keys = dot(ds, q)
    return d_keys, d_values, dot(keys, ds, ((0,), (0,)))


def diag_lanes(wide, n):
    return jnp.concatenate(
        [from_lanes(wide[HD * h:HD * h + HD], h, n, 0.0) for h in range(NH)], 0
    )


def half_mask(rows, h):
    return jnp.where((iota(rows.shape, 1) < HD) == (h % 2 == 0), rows.astype(F32), 0.0).astype(BF)


def half_pad(cols, h):
    zero = jnp.zeros_like(cols)
    return jnp.concatenate([cols, zero] if h % 2 == 0 else [zero, cols], 0)


def level1_backward(p, q_ref, q_t_ref, k_ref, k_t_ref, v_ref, g_ref, g_t_ref, lse_ref, delta_ref,
                    dk_ref, dv_ref, dq_ref):
    cols = slice(128 * p, 128 * p + 128)
    for h in (2 * p, 2 * p + 1):
        rows = slice(HD * h, HD * h + HD)
        for c in range(2):
            lanes = slice(256 * c, 256 * c + 256)
            q_t = half_pad(q_t_ref[rows, lanes], h)
            g_t = half_pad(g_t_ref[rows, lanes], h)
            prob = jnp.exp(dot(k_ref[:, cols], q_t) - lse_ref[h:h + 1, lanes])
            ds = (prob * (dot(v_ref[:, cols], g_t) - delta_ref[h:h + 1, lanes])).astype(BF)
            dv = dot(prob.astype(BF), half_mask(g_ref[lanes, cols], h))
            dk = dot(ds, half_mask(q_ref[lanes, cols], h))
            dq_ref[HD * (h % 2):HD * (h % 2) + HD, lanes] = dot(k_t_ref[rows, :], ds)
            if h % 2 == 0 and c == 0:
                dv_ref[...] = dv
                dk_ref[...] = dk
            else:
                dv_ref[...] += dv
                dk_ref[...] += dk


def pack1_kernel(pos, k, v, out):
    mats = [pick_mat(pos[0] * NH + m, SEL2) for m in range(NH)]
    ks, vs = per_head_rows(mats, [k[...], v[...]])
    out[0:SEL2] = ks.astype(BF)
    out[SEL2:2 * SEL2] = vs.astype(BF)


def first_kernel(pos, q, k, v, _p1, q_out, q_t_out, k_out, k_t_out, v_out, m_out, l_out, o_out):
    mats = [pick_mat(pos[0] * NH + m, T) for m in range(NH)]
    qs, ks, vs = per_head_rows(mats, [q[...], k[...], v[...]])
    qs = qs * SCALE
    q_out[...] = qs.astype(BF)
    q_t_out[...] = qs.T.astype(BF)
    k_out[...] = ks.astype(BF)
    k_t_out[...] = ks.T.astype(BF)
    v_out[...] = vs.astype(BF)
    v_t = vs.T.astype(BF)
    m_out[...] = jnp.zeros_like(m_out)
    l_out[...] = jnp.zeros_like(l_out)
    for h in range(NH):
        cols = slice(128 * (h // 2), 128 * (h // 2) + 128)
        rows = slice(HD * h, HD * h + HD)
        for c in range(2):
            lanes = slice(256 * c, 256 * c + 256)
            peak, total, weights = soft(dot(k_out[:, cols], half_pad(q_t_out[rows, lanes], h)))
            m_out[h:h + 1, lanes] = peak
            l_out[h:h + 1, lanes] = total
            o_out[rows, lanes] = dot(v_t[rows, :], weights)


def pack2_kernel(a0, a1, a2, a3, out):
    for n, a in enumerate((a0, a1, a2, a3)):
        out[SEL3 * n:SEL3 * n + SEL3] = a[0:SEL3]
        out[128 + SEL3 * n:128 + SEL3 * n + SEL3] = a[SEL2:SEL2 + SEL3]


def pack3_kernel(a0, a1, a2, a3, out):
    for base in (0, 128):
        parts = []
        for a in (a0, a1, a2, a3):
            for n in range(4):
                start = base + SEL3 * n
                parts.append(a[start:start + 16].astype(F32)[:SEL4])
        out[base:base + 128] = jnp.concatenate(parts, 0).astype(BF)


def stack_kv(refs):
    keys = jnp.concatenate([a[0:128] for a in refs], 0)
    values = jnp.concatenate([a[128:256] for a in refs], 0)
    return keys, values


def second_kernel(a0, a1, a2, a3, q, _p2, m_out, l_out, o_out):
    keys, values = stack_kv((a0, a1, a2, a3))
    _, q_t = blocks_both(q[0:SEL2].astype(F32), SEL2)
    peak, total, wide = forward(keys, values, q_t)
    m_out[...] = jnp.broadcast_to(peak, m_out.shape)
    l_out[...] = jnp.broadcast_to(total, l_out.shape)
    o_out[...] = jnp.concatenate(
        [wide[HD * h:HD * h + HD, 128 * h:128 * h + 128] for h in range(NH)], 0
    )


def third_kernel(pos, a0, a1, a2, a3, q, m1, l1, o1, m2, l2, o2, c0, c1, c2, c3, w, _p3,
                 m_out, l_out, o_out, g_out, g_t_out, lse_out, delta_out, att_out):
    here = pos[0]
    grad = None
    for r, c in enumerate((c0, c1, c2, c3)):
        at = pl.multiple_of((here ^ r) * F, F)
        term = dot(c[...], w[:, pl.ds(at, F)], ((1,), (1,)))
        grad = term if grad is None else grad + term
    mats = [pick_mat(here * NH + m, T) for m in range(NH)]
    (gs,) = per_head_rows(mats, [grad.astype(BF)])
    g_t = gs.T
    g_out[...] = gs.astype(BF)
    g_t_out[...] = g_t.astype(BF)

    keys, values = stack_kv((a0, a1, a2, a3))
    _, q_t = blocks_both(q[0:SEL3].astype(F32), SEL3)
    m3, l3, wide = forward(keys, values, q_t)
    m3 = jnp.broadcast_to(m3, (8, 128))
    l3 = jnp.broadcast_to(l3, (8, 128))
    lse_out[...] = jnp.zeros_like(lse_out)
    delta_out[...] = jnp.zeros_like(delta_out)
    m_out[...] = jnp.zeros_like(m_out)
    l_out[...] = jnp.zeros_like(l_out)
    for h in range(NH):
        rows = slice(HD * h, HD * h + HD)
        ma, la, oa = m1[h:h + 1, 0:128], l1[h:h + 1, 0:128], o1[rows, 0:128]
        mb, lb = m2[0:1, 128 * h:128 * h + 128], l2[0:1, 128 * h:128 * h + 128]
        mc = from_lanes(m3, h, SEL3, NEG)[0:1]
        lc = from_lanes(l3, h, SEL3, 0.0)[0:1]
        oc = from_lanes(wide[rows], h, SEL3, 0.0)
        top = jnp.maximum(jnp.maximum(ma, mb), mc)
        fa, fb, fc = jnp.exp(ma - top), jnp.exp(mb - top), jnp.exp(mc - top)
        m_out[h:h + 1] = top
        l_out[h:h + 1] = fa * la + fb * lb + fc * lc
        o_out[rows] = fa * oa + fb * o2[rows] + fc * oc
        total = l1[h:h + 1, 128:T]
        out = o1[rows, 128:T] / total
        lse_out[h:h + 1, 128:T] = m1[h:h + 1, 128:T] + jnp.log(total)
        delta_out[h:h + 1, 128:T] = jnp.sum(g_t_out[rows, 128:T].astype(F32) * out, axis=0, keepdims=True)
        att_out[rows] = dot(out.astype(BF), mats[h][128:T])


def fourth_kernel(pos, a0, a1, a2, a3, q, m, l, o, g, g_t, lse_in, delta_in, att_in, c0, c1, c2, c3,
                  lse_out, delta_out, att_out, dq_out, s0, s1, s2, s3, blocks):
    here, x_pos = pos[0], pos[1]
    keys, values = stack_kv((a0, a1, a2, a3))
    q4, q4_t = blocks_both(q[0:16].astype(F32), SEL4)
    g4, g4_t = blocks_both(g[0:16].astype(F32), SEL4)
    peak, total, weights = soft(dot(keys, q4_t))
    wide = dot(values, weights, ((0,), (0,)))
    peak = jnp.broadcast_to(peak, (8, 128))
    total = jnp.broadcast_to(total, (8, 128))
    lse_out[...] = lse_in[...]
    delta_out[...] = delta_in[...]
    lse_rows, delta_rows = [], []
    for h in range(NH):
        rows = slice(HD * h, HD * h + HD)
        ma, la, oa = m[h:h + 1], l[h:h + 1], o[rows]
        mb = from_lanes(peak, h, SEL4, NEG)[0:1]
        lb = from_lanes(total, h, SEL4, 0.0)[0:1]
        ob = from_lanes(wide[rows], h, SEL4, 0.0)
        top = jnp.maximum(ma, mb)
        fa, fb = jnp.exp(ma - top), jnp.exp(mb - top)
        denominator = fa * la + fb * lb
        out = (fa * oa + fb * ob) / denominator
        lse = top + jnp.log(denominator)
        delta = jnp.sum(g_t[rows, 0:128].astype(F32) * out, axis=0, keepdims=True)
        lse_out[h:h + 1, 0:128] = lse
        delta_out[h:h + 1, 0:128] = delta
        lse_rows.append(lse)
        delta_rows.append(delta)
        att = att_in[rows] + dot(out.astype(BF), pick_mat(here * NH + h, SEL2))
        att_out[rows] = att.astype(BF)
    d_keys, d_values, dq = backward(
        keys, values, q4, q4_t, g4, g4_t, to_lanes(lse_rows, SEL4), to_lanes(delta_rows, SEL4)
    )
    dq_out[...] = diag_lanes(dq, SEL4)
    for r, c in enumerate((c0, c1, c2, c3)):
        blocks[here ^ r] = c[...]
    for d, s in enumerate((s0, s1, s2, s3)):
        s[0:128] = d_keys[128 * d:128 * d + 128].astype(s.dtype)
        s[128:256] = d_values[128 * d:128 * d + 128].astype(s.dtype)
        term = dot(att_out[...], blocks[(x_pos - d) & 3])
        s[256:512] = term.T.astype(s.dtype)


def project_kernel(pos, att, w, send, keep_a, keep_b):
    here = pos[0]
    for r, ref in ((0, keep_a), (2, keep_b), (1, send.at[0:T]), (3, send.at[T:2 * T])):
        at = pl.multiple_of((here ^ r) * F, F)
        ref[...] = dot(att[...], w[:, pl.ds(at, F)], ((0,), (0,))).astype(ref.dtype)


def fifth_kernel(a0, a1, a2, a3, q, q_t, k, k_t, v, g, g_t, lse, delta, dq_in,
                 dk3, dv3, dq_first, dk, dv, dq):
    keys, values = stack_kv((a0, a1, a2, a3))
    q3, q3_t = blocks_both(q[0:SEL3].astype(F32), SEL3)
    g3, g3_t = blocks_both(g[0:SEL3].astype(F32), SEL3)
    lse3 = to_lanes([lse[h:h + 1, 0:128] for h in range(NH)], SEL3)
    delta3 = to_lanes([delta[h:h + 1, 0:128] for h in range(NH)], SEL3)
    dk3[...], dv3[...], wide = backward(keys, values, q3, q3_t, g3, g3_t, lse3, delta3)
    dq_first[...] = dq_in[...] + diag_lanes(wide, SEL3)
    level1_backward(0, q, q_t, k, k_t, v, g, g_t, lse, delta, dk, dv, dq)


def reduce_z_kernel(pos, own, b1, b2, b3, dk3, dv3, s0, s1, s2, s3, total):
    z_pos = pos[2]
    total[...] = own[...] + b1[...].astype(F32) + b2[...].astype(F32) + b3[...].astype(F32)
    for d, s in enumerate((s0, s1, s2, s3)):
        for base, level in ((0, dk3), (128, dv3)):
            parts = []
            for n in range(4):
                at = 128 * d + SEL3 * n
                start = base + SEL3 * d + SEL4 * n
                parts.append(level[at:at + SEL4] + total[start:start + SEL4])
                parts.append(level[at + SEL4:at + SEL3])
            s[base:base + 128] = jnp.concatenate(parts, 0).astype(s.dtype)
        start = pl.multiple_of(256 + 64 * ((z_pos - d) & 3), 64)
        s[256:320] = total[pl.ds(start, 64)].astype(s.dtype)


def sixth_kernel(a0, a1, a2, a3, q, g, lse, delta, dq_in, _s, dk2, dv2, dq_first):
    keys, values = stack_kv((a0, a1, a2, a3))
    q2, q2_t = blocks_both(q[0:SEL2].astype(F32), SEL2)
    g2, g2_t = blocks_both(g[0:SEL2].astype(F32), SEL2)
    lse2 = jnp.concatenate([lse[h:h + 1, 0:128] for h in range(NH)], 1)
    delta2 = jnp.concatenate([delta[h:h + 1, 0:128] for h in range(NH)], 1)
    dk2[...], dv2[...], wide = backward(keys, values, q2, q2_t, g2, g2_t, lse2, delta2)
    diag = [wide[HD * h:HD * h + HD, 128 * h:128 * h + 128] for h in range(NH)]
    dq_first[...] = dq_in[...] + jnp.concatenate(diag, 0)


def reduce_y_kernel(pos, own, b1, b2, b3, dk2, dv2, s0, s1, s2, s3, total):
    y_pos = pos[3]
    total[...] = own[...] + b1[...].astype(F32) + b2[...].astype(F32) + b3[...].astype(F32)
    for d, s in enumerate((s0, s1, s2, s3)):
        for base, level in ((0, dk2), (128, dv2)):
            at = 128 * d
            start = base + SEL3 * d
            s[base:base + SEL3] = (level[at:at + SEL3] + total[start:start + SEL3]).astype(s.dtype)
            s[base + SEL3:base + 128] = level[at + SEL3:at + 128].astype(s.dtype)
        start = pl.multiple_of(256 + 16 * ((y_pos - d) & 3), 16)
        s[256:272] = total[pl.ds(start, 16)].astype(s.dtype)


def mix_kernel(keep_a, keep_b, got, own, send):
    own[...] = keep_a[...] + got[0:T].astype(F32)
    send[...] = (keep_b[...] + got[T:2 * T].astype(F32)).astype(BF)


def seventh_kernel(pos, q, q_t, k, k_t, v, g, g_t, lse, delta, dq_first, dk_a, dv_a, dq_a, _s,
                   dq_out, dk_part, dv_part, dk_head, dv_head, dk, dv, dq):
    level1_backward(1, q, q_t, k, k_t, v, g, g_t, lse, delta, dk, dv, dq)
    for p, (dk_p, dv_p, dq_p) in enumerate(((dk_a, dv_a, dq_a), (dk, dv, dq))):
        cols = slice(128 * p, 128 * p + 128)
        dk_head[:, cols] = dk_p[0:SEL2]
        dv_head[:, cols] = dv_p[0:SEL2]
        first = dq_p[:, 0:128] + dq_first[cols]
        dq_t = jnp.concatenate([first, dq_p[:, 128:T]], 1) * SCALE
        later = jnp.concatenate([dk_p[SEL2:T], dv_p[SEL2:T]], 1).astype(BF)
        both = jnp.concatenate([jnp.zeros((SEL2, 256), BF), later], 0)
        both = jnp.concatenate([both, dq_t.T.astype(BF)], 1)
        even = dot(put_mat(pos[0] * NH + 2 * p, T), both)
        odd = dot(put_mat(pos[0] * NH + 2 * p + 1, T), both)
        natural = jnp.where((iota(even.shape, 1) & 127) < HD, even, odd)
        dk_part[:, cols] = natural[:, 0:128].astype(BF)
        dv_part[:, cols] = natural[:, 128:256].astype(BF)
        dq_out[:, cols] = natural[:, 256:384].astype(BF)


def last_kernel(pos, own, b1, b2, b3, dk_head, dv_head, dk_part, dv_part, mix_own, mix_got,
                dk_out, dv_out, w_out, mixed_out):
    total = own[...] + b1[...].astype(F32) + b2[...].astype(F32) + b3[...].astype(F32)
    ks = (total[0:128] + dk_head[...]).astype(BF)
    vs = (total[128:256] + dv_head[...]).astype(BF)
    w_out[...] = total[256:272].T
    mats = [put_mat(pos[0] * NH + m, SEL2) for m in range(NH)]
    ks, vs = per_head_rows(mats, [ks, vs])
    dk_out[...] = (ks + dk_part[...].astype(F32)).astype(BF)
    dv_out[...] = (vs + dv_part[...].astype(F32)).astype(BF)
    mixed_out[...] = (mix_own[...] + mix_got[...].astype(F32)).astype(BF)


def call(kernel, outs, *args, us=5, scratch=()):
    def spec(arg):
        return pl.BlockSpec(memory_space=pltpu.SMEM if arg.dtype == jnp.int32 else pltpu.VMEM)

    return pl.pallas_call(
        kernel,
        out_shape=[jax.ShapeDtypeStruct(shape, dtype) for shape, dtype in outs],
        in_specs=[spec(a) for a in args],
        out_specs=[pl.BlockSpec(memory_space=pltpu.VMEM)] * len(outs),
        scratch_shapes=scratch,
        compiler_params=pltpu.CompilerParams(vmem_limit_bytes=40 * 2 ** 20),
        cost_estimate=pl.CostEstimate(flops=us * 500_000_000, bytes_accessed=us * 1_000_000, transcendentals=0),
        name=kernel.__name__,
    )(*args)


def step(stride, shift):
    pairs = []
    for s in range(64):
        at = s // stride % 4
        pairs.append((s, s + ((at + shift) % 4 - at) * stride))
    return pairs


def spread(block, stride):
    return [block] + [lax.ppermute(block, "seq", step(stride, d)) for d in (1, 2, 3)]


def bring(blocks, stride):
    return [blocks[0]] + [lax.ppermute(blocks[d], "seq", step(stride, -d)) for d in (1, 2, 3)]


def swap(block, mask):
    return lax.ppermute(block, "head", [(s, s ^ mask) for s in range(4)])


def body(query_act, key_act, value_act, out_weight, cotangent):
    seq = lax.axis_index("seq")
    head = lax.axis_index("head")
    pos = jnp.stack([head, seq // 16, seq // 4 % 4, seq % 4]).astype(jnp.int32)
    wide, tall, stat = (T, F), (F, T), (8, T)

    (p1,) = call(pack1_kernel, [((256, F), BF)], pos, key_act, value_act, us=2)
    kv2 = spread(p1, 1)
    cot_z = swap(cotangent, 2)
    cot_c = swap(cotangent, 1)
    cot_zc = swap(cot_z, 1)
    cots = [cotangent, cot_c, cot_z, cot_zc]

    q, q_t, k, k_t, v, m1, l1, o1 = call(
        first_kernel,
        [(wide, BF), (tall, BF), (wide, BF), (tall, BF), (wide, BF), (stat, F32), (stat, F32), (tall, F32)],
        pos, query_act, key_act, value_act, p1, us=10,
    )
    (p2,) = call(pack2_kernel, [((256, F), BF)], *kv2, us=1)
    kv3 = spread(p2, 4)
    m2, l2, o2 = call(
        second_kernel, [(stat, F32), (stat, F32), ((F, 128), F32)], *kv2, q, p2, us=6
    )
    (p3,) = call(pack3_kernel, [((256, F), BF)], *kv3, us=1)
    kv4 = spread(p3, 16)
    m, l, o, g, g_t, lse, delta, att_part = call(
        third_kernel,
        [((8, 128), F32), ((8, 128), F32), ((F, 128), F32), (wide, BF), (tall, BF), (stat, F32), (stat, F32),
         (tall, F32)],
        pos, *kv3, q, m1, l1, o1, m2, l2, o2, *cots, out_weight, p3, us=8,
    )
    lse, delta, att, dq4, *sent = call(
        fourth_kernel,
        [(stat, F32), (stat, F32), (tall, BF), ((F, 128), F32), ((512, F), F32)] + [((512, F), BF)] * 3,
        pos, *kv4, q, m, l, o, g, g_t, lse, delta, att_part, *cots, us=6,
        scratch=[pltpu.VMEM((4, T, F), BF)],
    )
    r4 = bring(sent, 16)
    send_c, keep_a, keep_b = call(
        project_kernel, [((2 * T, F), BF), (wide, F32), (wide, F32)], pos, att, out_weight, us=2
    )
    got_c = swap(send_c, 1)
    dk3, dv3, dq_first, dk_a, dv_a, dq_a = call(
        fifth_kernel,
        [(wide, F32), (wide, F32), ((F, 128), F32), ((T, 128), F32), ((T, 128), F32), ((128, T), F32)],
        *kv3, q, q_t, k, k_t, v, g, g_t, lse, delta, dq4, us=10,
    )
    *sent, _ = call(
        reduce_z_kernel, [((320, F), F32)] + [((320, F), BF)] * 3 + [((512, F), F32)],
        pos, *r4, dk3, dv3, us=1,
    )
    r3 = bring(sent, 4)
    mix_own, mix_send = call(mix_kernel, [(wide, F32), (wide, BF)], keep_a, keep_b, got_c, us=1)
    mix_got = swap(mix_send, 2)
    dk2, dv2, dq_first = call(
        sixth_kernel, [(wide, F32), (wide, F32), ((F, 128), F32)],
        *kv2, q, g, lse, delta, dq_first, sent[1], us=7,
    )
    *sent, _ = call(
        reduce_y_kernel, [((272, F), F32)] + [((272, F), BF)] * 3 + [((320, F), F32)],
        pos, *r3, dk2, dv2, us=1,
    )
    r2 = bring(sent, 1)
    query_grad, dk_part, dv_part, dk_head, dv_head, *_ = call(
        seventh_kernel,
        [(wide, BF), (wide, BF), (wide, BF), ((SEL2, F), F32), ((SEL2, F), F32),
         ((T, 128), F32), ((T, 128), F32), ((128, T), F32)],
        pos, q, q_t, k, k_t, v, g, g_t, lse, delta, dq_first, dk_a, dv_a, dq_a, sent[1], us=9,
    )
    key_grad, value_grad, weight_grad, mixed_out = call(
        last_kernel, [(wide, BF), (wide, BF), ((F, 16), F32), (wide, BF)],
        pos, *r2, dk_head, dv_head, dk_part, dv_part, mix_own, mix_got, us=2,
    )
    return mixed_out, query_grad, key_grad, value_grad, weight_grad


def solution(mesh):
    rows = P("seq", "head")
    return jax.shard_map(
        body,
        mesh=mesh,
        in_specs=(rows, rows, rows, P("head", None), rows),
        out_specs=(rows, rows, rows, rows, P("head", "seq")),
        check_vma=False,
    )
```

```python
import functools

import functools

import jax
import jax.numpy as jnp
from jax import lax
from jax.experimental import pallas as pl
from jax.experimental.pallas import tpu as pltpu
from jax.sharding import PartitionSpec as P

HD = 64
NH = 4
T = 512
F = NH * HD
SEL2, SEL3, SEL4 = 128, 32, 8
SCALE = HD ** -0.5
NEG = -1e30
BF = jnp.bfloat16
F32 = jnp.float32


def iota(shape, dim):
    return lax.broadcasted_iota(jnp.int32, shape, dim)


def token_of(index):
    return (index >> 7) + ((index >> 5) & 3) * 4 + ((index >> 3) & 3) * 16 + (index & 7) * 64


def pick_mat(head, rows):
    wanted = (token_of(iota((rows, T), 0)) + head) & (T - 1)
    return jnp.where(wanted == iota((rows, T), 1), 1.0, 0.0).astype(BF)


def put_mat(head, cols):
    wanted = (token_of(iota((T, cols), 1)) + head) & (T - 1)
    return jnp.where(wanted == iota((T, cols), 0), 1.0, 0.0).astype(BF)


def dot(a, b, dims=((1,), (0,))):
    return lax.dot_general(a, b, (dims, ((), ())), preferred_element_type=F32)


def per_head_rows(mats, arrays):
    pairs = []
    for p in range(2):
        both = jnp.concatenate([a[:, 128 * p:128 * p + 128] for a in arrays], 1)
        even = dot(mats[2 * p], both)
        odd = dot(mats[2 * p + 1], both)
        pairs.append(jnp.where((iota(even.shape, 1) & 127) < HD, even, odd))
    return [
        jnp.concatenate([pair[:, 128 * n:128 * n + 128] for pair in pairs], 1)
        for n in range(len(arrays))
    ]


def head_blocks(rows, n):
    part = rows[:n]
    lane_head = iota(part.shape, 1) >> 6
    return jnp.concatenate([jnp.where(lane_head == h, part, 0.0) for h in range(NH)], 0)


def blocks_both(rows, n):
    full = head_blocks(rows, n)
    if NH * n < 128:
        full = jnp.concatenate([full, jnp.zeros((128 - NH * n, F), F32)], 0)
    return full.astype(BF), full.T.astype(BF)


def to_lanes(rows, n):
    total = None
    for h in range(NH):
        row = jnp.broadcast_to(jnp.where(iota((1, 128), 1) < n, rows[h], 0.0), (8, 128))
        if h:
            row = pltpu.roll(row, n * h, 1)
        total = row if total is None else total + row
    return total[0:1]


def from_lanes(rows, h, n, fill):
    if h:
        rows = pltpu.roll(rows, 128 - n * h, 1)
    return jnp.where(iota(rows.shape, 1) < n, rows, fill)


def soft(scores):
    peak = jnp.max(scores, axis=0, keepdims=True)
    weights = jnp.exp(scores - peak)
    return peak, jnp.sum(weights, axis=0, keepdims=True), weights.astype(BF)


def forward(keys, values, q_t):
    peak, total, weights = soft(dot(keys, q_t))
    return peak, total, dot(values, weights, ((0,), (0,)))


def backward(keys, values, q, q_t, g, g_t, lse, delta):
    prob = jnp.exp(dot(keys, q_t) - lse)
    ds = (prob * (dot(values, g_t) - delta)).astype(BF)
    d_values = dot(prob.astype(BF), g)
    d_keys = dot(ds, q)
    return d_keys, d_values, dot(keys, ds, ((0,), (0,)))


def diag_lanes(wide, n):
    return jnp.concatenate(
        [from_lanes(wide[HD * h:HD * h + HD], h, n, 0.0) for h in range(NH)], 0
    )


def half_mask(rows, h):
    return jnp.where((iota(rows.shape, 1) < HD) == (h % 2 == 0), rows.astype(F32), 0.0).astype(BF)


def half_pad(cols, h):
    zero = jnp.zeros_like(cols)
    return jnp.concatenate([cols, zero] if h % 2 == 0 else [zero, cols], 0)


def level1_backward(p, q_ref, q_t_ref, k_ref, k_t_ref, v_ref, g_ref, g_t_ref, lse_ref, delta_ref,
                    dk_ref, dv_ref, dq_ref):
    cols = slice(128 * p, 128 * p + 128)
    for h in (2 * p, 2 * p + 1):
        rows = slice(HD * h, HD * h + HD)
        for c in range(2):
            lanes = slice(256 * c, 256 * c + 256)
            q_t = half_pad(q_t_ref[rows, lanes], h)
            g_t = half_pad(g_t_ref[rows, lanes], h)
            prob = jnp.exp(dot(k_ref[:, cols], q_t) - lse_ref[h:h + 1, lanes])
            ds = (prob * (dot(v_ref[:, cols], g_t) - delta_ref[h:h + 1, lanes])).astype(BF)
            dv = dot(prob.astype(BF), half_mask(g_ref[lanes, cols], h))
            dk = dot(ds, half_mask(q_ref[lanes, cols], h))
            dq_ref[HD * (h % 2):HD * (h % 2) + HD, lanes] = dot(k_t_ref[rows, :], ds)
            if h % 2 == 0 and c == 0:
                dv_ref[...] = dv
                dk_ref[...] = dk
            else:
                dv_ref[...] += dv
                dk_ref[...] += dk


def pick3_kernel(pos, k, v, out):
    mats = [pick_mat(pos[0] * NH + m, SEL3) for m in range(NH)]
    ks, vs = per_head_rows(mats, [k[...], v[...]])
    out[0:SEL3] = ks.astype(BF)
    out[SEL3:2 * SEL3] = vs.astype(BF)


def pick2_kernel(pos, k, v, _p3, out):
    mats = [pick_mat(pos[0] * NH + m, SEL2) for m in range(NH)]
    ks, vs = per_head_rows(mats, [k[...], v[...]])
    out[0:SEL2] = ks.astype(BF)
    out[SEL2:2 * SEL2] = vs.astype(BF)


def order_kernel(pos, q, k, v, _s, q_out, q_t_out, k_out, k_t_out, v_out, v_t_out):
    mats = [pick_mat(pos[0] * NH + m, T) for m in range(NH)]
    qs, ks, vs = per_head_rows(mats, [q[...], k[...], v[...]])
    qs = qs * SCALE
    q_out[...] = qs.astype(BF)
    q_t_out[...] = qs.T.astype(BF)
    k_out[...] = ks.astype(BF)
    k_t_out[...] = ks.T.astype(BF)
    v_out[...] = vs.astype(BF)
    v_t_out[...] = vs.T.astype(BF)


def first_kernel(p, q_t, k, v_t, _s, m_out, l_out, o_out):
    m_out[...] = jnp.zeros_like(m_out)
    l_out[...] = jnp.zeros_like(l_out)
    cols = slice(128 * p, 128 * p + 128)
    for h in range(2):
        rows_in = slice(HD * (2 * p + h), HD * (2 * p + h) + HD)
        rows = slice(HD * h, HD * h + HD)
        for c in range(2):
            lanes = slice(256 * c, 256 * c + 256)
            peak, total, weights = soft(dot(k[:, cols], half_pad(q_t[rows_in, lanes], h)))
            m_out[h:h + 1, lanes] = peak
            l_out[h:h + 1, lanes] = total
            o_out[rows, lanes] = dot(v_t[rows_in, :], weights)


def pair_kernel(a, b, _s, out):
    rows = a.shape[0]
    out[0:rows] = a[...]
    out[rows:2 * rows] = b[...]


def pack3_kernel(a, b, c, cot, _s, out, cot_out):
    cot_out[...] = cot[...]
    for half in range(2):
        base = SEL3 * half
        rows = [a[base:base + SEL3], b[base:base + SEL3], c[64 + base:64 + base + SEL3], c[base:base + SEL3]]
        for n, part in enumerate(rows):
            out[128 * half + SEL3 * n:128 * half + SEL3 * n + SEL3] = part


def pack4_kernel(a0, a1, a2, a3, _s, _t, out):
    for base in (0, 128):
        parts = []
        for a in (a0, a1, a2, a3):
            for n in range(4):
                start = base + SEL3 * n
                parts.append(a[start:start + 16].astype(F32)[:SEL4])
        out[base:base + 128] = jnp.concatenate(parts, 0).astype(BF)


def stack_kv(refs):
    keys = jnp.concatenate([a[0:128] for a in refs], 0)
    values = jnp.concatenate([a[128:256] for a in refs], 0)
    return keys, values


def second_kernel(a, b, q, m_out, l_out, o_out):
    keys, values = stack_kv((a.at[0:256], a.at[256:512], b.at[0:256], b.at[256:512]))
    _, q_t = blocks_both(q[0:SEL2].astype(F32), SEL2)
    peak, total, wide = forward(keys, values, q_t)
    m_out[...] = jnp.broadcast_to(peak, m_out.shape)
    l_out[...] = jnp.broadcast_to(total, l_out.shape)
    o_out[...] = jnp.concatenate(
        [wide[HD * h:HD * h + HD, 128 * h:128 * h + 128] for h in range(NH)], 0
    )


def third_kernel(pos, a0, a1, a2, a3, q, m1a, l1a, o1a, m1b, l1b, o1b, m2, l2, o2, c0, c1, c2, c3, w, _p3,
                 m_out, l_out, o_out, g_out, g_t_out, lse_out, delta_out, att_out):
    here = pos[0]
    grad = None
    for r, c in enumerate((c0, c1, c2, c3)):
        at = pl.multiple_of((here ^ r) * F, F)
        term = dot(c[...], w[:, pl.ds(at, F)], ((1,), (1,)))
        grad = term if grad is None else grad + term
    mats = [pick_mat(here * NH + m, T) for m in range(NH)]
    (gs,) = per_head_rows(mats, [grad.astype(BF)])
    g_t = gs.T
    g_out[...] = gs.astype(BF)
    g_t_out[...] = g_t.astype(BF)

    keys, values = stack_kv((a0, a1, a2, a3))
    _, q_t = blocks_both(q[0:SEL3].astype(F32), SEL3)
    m3, l3, wide = forward(keys, values, q_t)
    m3 = jnp.broadcast_to(m3, (8, 128))
    l3 = jnp.broadcast_to(l3, (8, 128))
    lse_out[...] = jnp.zeros_like(lse_out)
    delta_out[...] = jnp.zeros_like(delta_out)
    m_out[...] = jnp.zeros_like(m_out)
    l_out[...] = jnp.zeros_like(l_out)
    for h in range(NH):
        rows = slice(HD * h, HD * h + HD)
        m1, l1, o1 = ((m1a, l1a, o1a), (m1b, l1b, o1b))[h // 2]
        one, half = slice(h % 2, h % 2 + 1), slice(HD * (h % 2), HD * (h % 2) + HD)
        ma, la, oa = m1[one, 0:128], l1[one, 0:128], o1[half, 0:128]
        mb, lb = m2[0:1, 128 * h:128 * h + 128], l2[0:1, 128 * h:128 * h + 128]
        mc = from_lanes(m3, h, SEL3, NEG)[0:1]
        lc = from_lanes(l3, h, SEL3, 0.0)[0:1]
        oc = from_lanes(wide[rows], h, SEL3, 0.0)
        top = jnp.maximum(jnp.maximum(ma, mb), mc)
        fa, fb, fc = jnp.exp(ma - top), jnp.exp(mb - top), jnp.exp(mc - top)
        m_out[h:h + 1] = top
        l_out[h:h + 1] = fa * la + fb * lb + fc * lc
        o_out[rows] = fa * oa + fb * o2[rows] + fc * oc
        total = l1[one, 128:T]
        out = o1[half, 128:T] / total
        lse_out[h:h + 1, 128:T] = m1[one, 128:T] + jnp.log(total)
        delta_out[h:h + 1, 128:T] = jnp.sum(g_t_out[rows, 128:T].astype(F32) * out, axis=0, keepdims=True)
        att_out[rows] = dot(out.astype(BF), mats[h][128:T])


def fourth_kernel(pos, a0, a1, a2, a3, q, m, l, o, g, g_t, lse_in, delta_in, att_in, c0, c1, c2, c3,
                  lse_out, delta_out, att_out, dq_out, s0, s1, s2, s3, blocks):
    here, x_pos = pos[0], pos[1]
    keys, values = stack_kv((a0, a1, a2, a3))
    q4, q4_t = blocks_both(q[0:16].astype(F32), SEL4)
    g4, g4_t = blocks_both(g[0:16].astype(F32), SEL4)
    peak, total, weights = soft(dot(keys, q4_t))
    wide = dot(values, weights, ((0,), (0,)))
    peak = jnp.broadcast_to(peak, (8, 128))
    total = jnp.broadcast_to(total, (8, 128))
    lse_out[...] = lse_in[...]
    delta_out[...] = delta_in[...]
    lse_rows, delta_rows = [], []
    for h in range(NH):
        rows = slice(HD * h, HD * h + HD)
        ma, la, oa = m[h:h + 1], l[h:h + 1], o[rows]
        mb = from_lanes(peak, h, SEL4, NEG)[0:1]
        lb = from_lanes(total, h, SEL4, 0.0)[0:1]
        ob = from_lanes(wide[rows], h, SEL4, 0.0)
        top = jnp.maximum(ma, mb)
        fa, fb = jnp.exp(ma - top), jnp.exp(mb - top)
        denominator = fa * la + fb * lb
        out = (fa * oa + fb * ob) / denominator
        lse = top + jnp.log(denominator)
        delta = jnp.sum(g_t[rows, 0:128].astype(F32) * out, axis=0, keepdims=True)
        lse_out[h:h + 1, 0:128] = lse
        delta_out[h:h + 1, 0:128] = delta
        lse_rows.append(lse)
        delta_rows.append(delta)
        att = att_in[rows] + dot(out.astype(BF), pick_mat(here * NH + h, SEL2))
        att_out[rows] = att.astype(BF)
    d_keys, d_values, dq = backward(
        keys, values, q4, q4_t, g4, g4_t, to_lanes(lse_rows, SEL4), to_lanes(delta_rows, SEL4)
    )
    dq_out[...] = diag_lanes(dq, SEL4)
    for r, c in enumerate((c0, c1, c2, c3)):
        blocks[here ^ r] = c[...]
    for d, s in enumerate((s0, s1, s2, s3)):
        s[0:128] = d_keys[128 * d:128 * d + 128].astype(s.dtype)
        s[128:256] = d_values[128 * d:128 * d + 128].astype(s.dtype)
        term = dot(att_out[...], blocks[(x_pos - d) & 3])
        s[256:512] = term.T.astype(s.dtype)


def project_kernel(pos, att, w, _s, send, keep_a, keep_b):
    here = pos[0]
    for r, ref in ((0, keep_a), (2, keep_b), (1, send.at[0:T]), (3, send.at[T:2 * T])):
        at = pl.multiple_of((here ^ r) * F, F)
        ref[...] = dot(att[...], w[:, pl.ds(at, F)], ((0,), (0,))).astype(ref.dtype)


def second_back_kernel(a, b, q, g, lse, delta, dq_in, own, send, dq_first):
    keys, values = stack_kv((a.at[0:256], a.at[256:512], b.at[0:256], b.at[256:512]))
    q2, q2_t = blocks_both(q[0:SEL2].astype(F32), SEL2)
    g2, g2_t = blocks_both(g[0:SEL2].astype(F32), SEL2)
    lse2 = jnp.concatenate([lse[h:h + 1, 0:128] for h in range(NH)], 1)
    delta2 = jnp.concatenate([delta[h:h + 1, 0:128] for h in range(NH)], 1)
    d_keys, d_values, wide = backward(keys, values, q2, q2_t, g2, g2_t, lse2, delta2)
    diag = [wide[HD * h:HD * h + HD, 128 * h:128 * h + 128] for h in range(NH)]
    dq_first[...] = dq_in[...] + jnp.concatenate(diag, 0)
    for n, (out, at) in enumerate(((own, 0), (own, 256), (send, 0), (send, 256))):
        out[at:at + 128] = d_keys[128 * n:128 * n + 128].astype(out.dtype)
        out[at + 128:at + 256] = d_values[128 * n:128 * n + 128].astype(out.dtype)


def fold_kernel(own, got, keep, send):
    keep[...] = own[0:256] + got[0:256].astype(F32)
    send[...] = (own[256:512] + got[256:512].astype(F32)).astype(BF)


def third_back_kernel(a0, a1, a2, a3, q, q_t, k, k_t, v, g, g_t, lse, delta, dq_in,
                      dk3, dv3, dq_first, dk, dv, dq):
    keys, values = stack_kv((a0, a1, a2, a3))
    q3, q3_t = blocks_both(q[0:SEL3].astype(F32), SEL3)
    g3, g3_t = blocks_both(g[0:SEL3].astype(F32), SEL3)
    lse3 = to_lanes([lse[h:h + 1, 0:128] for h in range(NH)], SEL3)
    delta3 = to_lanes([delta[h:h + 1, 0:128] for h in range(NH)], SEL3)
    dk3[...], dv3[...], wide = backward(keys, values, q3, q3_t, g3, g3_t, lse3, delta3)
    dq_first[...] = dq_in[...] + diag_lanes(wide, SEL3)
    level1_backward(0, q, q_t, k, k_t, v, g, g_t, lse, delta, dk, dv, dq)


def pair_back_kernel(q, q_t, k, k_t, v, g, g_t, lse, delta, _s, dk, dv, dq):
    level1_backward(1, q, q_t, k, k_t, v, g, g_t, lse, delta, dk, dv, dq)


def reduce_y_kernel(pos, own, b1, b2, b3, dk3, dv3, _s, s0, s1, s2, s3, total):
    y_pos = pos[3]
    total[...] = own[...] + b1[...].astype(F32) + b2[...].astype(F32) + b3[...].astype(F32)
    for d, s in enumerate((s0, s1, s2, s3)):
        for base, level in ((0, dk3), (128, dv3)):
            parts = []
            for n in range(4):
                at = 128 * d + SEL3 * n
                start = base + SEL3 * d + SEL4 * n
                parts.append(level[at:at + SEL4] + total[start:start + SEL4])
                parts.append(level[at + SEL4:at + SEL3])
            s[base:base + 128] = jnp.concatenate(parts, 0).astype(s.dtype)
        for n in range(4):
            start = pl.multiple_of(256 + 64 * n + 16 * ((y_pos - d) & 3), 16)
            s[256 + 16 * n:272 + 16 * n] = total[pl.ds(start, 16)].astype(s.dtype)


def reduce_z_kernel(pos, own, b1, b2, b3, s0, s1, s2, s3, total):
    z_pos = pos[2]
    total[...] = own[...] + b1[...].astype(F32) + b2[...].astype(F32) + b3[...].astype(F32)
    for d, s in enumerate((s0, s1, s2, s3)):
        s[0:SEL3] = total[SEL3 * d:SEL3 * d + SEL3].astype(s.dtype)
        s[SEL3:2 * SEL3] = total[128 + SEL3 * d:128 + SEL3 * d + SEL3].astype(s.dtype)
        start = pl.multiple_of(256 + 16 * (z_pos ^ d), 16)
        s[64:80] = total[pl.ds(start, 16)].astype(s.dtype)


def mix_kernel(keep_a, keep_b, got, own, send):
    own[...] = keep_a[...] + got[0:T].astype(F32)
    send[...] = (keep_b[...] + got[T:2 * T].astype(F32)).astype(BF)


def natural_kernel(pos, dq_first, dk_a, dv_a, dq_a, dk_b, dv_b, dq_b, own2, got2, mix_own, mix_got, _s,
                   dq_out, dk_part, dv_part, dk_head, dv_head, mixed_out):
    level2 = own2[...] + got2[...].astype(F32)
    mixed_out[...] = (mix_own[...] + mix_got[...].astype(F32)).astype(BF)
    for p, (dk, dv, dq) in enumerate(((dk_a, dv_a, dq_a), (dk_b, dv_b, dq_b))):
        cols = slice(128 * p, 128 * p + 128)
        dk_top = dk[0:SEL2] + level2[0:SEL2, cols]
        dv_top = dv[0:SEL2] + level2[SEL2:2 * SEL2, cols]
        dk_head[:, cols] = dk_top[0:SEL3]
        dv_head[:, cols] = dv_top[0:SEL3]
        dq_t = jnp.concatenate([dq[:, 0:128] + dq_first[cols], dq[:, 128:T]], 1) * SCALE
        later = [
            jnp.concatenate([jnp.zeros((SEL3, 128), F32), top[SEL3:SEL2], rest[SEL2:T]], 0)
            for top, rest in ((dk_top, dk), (dv_top, dv))
        ]
        both = jnp.concatenate(later + [dq_t.T], 1).astype(BF)
        even = dot(put_mat(pos[0] * NH + 2 * p, T), both)
        odd = dot(put_mat(pos[0] * NH + 2 * p + 1, T), both)
        natural = jnp.where((iota(even.shape, 1) & 127) < HD, even, odd)
        dk_part[:, cols] = natural[:, 0:128].astype(BF)
        dv_part[:, cols] = natural[:, 128:256].astype(BF)
        dq_out[:, cols] = natural[:, 256:384].astype(BF)


def last_kernel(pos, own, b1, b2, b3, dk_head, dv_head, dk_part, dv_part, dk_out, dv_out, w_out):
    total = own[...] + b1[...].astype(F32) + b2[...].astype(F32) + b3[...].astype(F32)
    ks = (total[0:SEL3] + dk_head[...]).astype(BF)
    vs = (total[SEL3:2 * SEL3] + dv_head[...]).astype(BF)
    w_out[...] = total[64:80]
    mats = [put_mat(pos[0] * NH + m, SEL3) for m in range(NH)]
    ks, vs = per_head_rows(mats, [ks, vs])
    dk_out[...] = (ks + dk_part[...].astype(F32)).astype(BF)
    dv_out[...] = (vs + dv_part[...].astype(F32)).astype(BF)


def call(kernel, outs, *args, us=5, scratch=()):
    def spec(arg):
        return pl.BlockSpec(memory_space=pltpu.SMEM if arg.dtype == jnp.int32 else pltpu.VMEM)

    return pl.pallas_call(
        kernel,
        out_shape=[jax.ShapeDtypeStruct(shape, dtype) for shape, dtype in outs],
        in_specs=[spec(a) for a in args],
        out_specs=[pl.BlockSpec(memory_space=pltpu.VMEM)] * len(outs),
        scratch_shapes=scratch,
        compiler_params=pltpu.CompilerParams(vmem_limit_bytes=24 * 2 ** 20),
        cost_estimate=pl.CostEstimate(flops=us * 500_000_000, bytes_accessed=us * 1_000_000, transcendentals=0),
        name=getattr(kernel, "func", kernel).__name__,
    )(*args)


def step(stride, shift):
    pairs = []
    for s in range(64):
        at = s // stride % 4
        pairs.append((s, s + ((at + shift) % 4 - at) * stride))
    return pairs


def spread(block, stride):
    return [block] + [lax.ppermute(block, "seq", step(stride, d)) for d in (1, 2, 3)]


def bring(blocks, stride):
    return [blocks[0]] + [lax.ppermute(blocks[d], "seq", step(stride, -d)) for d in (1, 2, 3)]


def swap_z(block, mask):
    return lax.ppermute(block, "seq", [(s, s ^ (4 * mask)) for s in range(64)])


def swap_y(block, mask):
    return lax.ppermute(block, "seq", [(s, s ^ mask) for s in range(64)])


def swap(block, mask):
    return lax.ppermute(block, "head", [(s, s ^ mask) for s in range(4)])


def body(query_act, key_act, value_act, out_weight, cotangent):
    seq = lax.axis_index("seq")
    head = lax.axis_index("head")
    pos = jnp.stack([head, seq // 16, seq // 4 % 4, seq % 4]).astype(jnp.int32)
    wide, tall, stat = (T, F), (F, T), (8, T)

    (mine3,) = call(pick3_kernel, [((64, F), BF)], pos, key_act, value_act, us=1)
    pair_a = swap_z(mine3, 1)
    (mine2,) = call(pick2_kernel, [((256, F), BF)], pos, key_act, value_act, mine3, us=1)
    got2 = swap_y(mine2, 1)
    q, q_t, k, k_t, v, v_t = call(
        order_kernel, [(wide, BF), (tall, BF)] * 3, pos, query_act, key_act, value_act, mine2, us=3,
    )
    (both,) = call(pair_kernel, [((128, F), BF)], mine3, pair_a, q, us=1)
    pair_b = swap_z(both, 3)
    (half2,) = call(pair_kernel, [((512, F), BF)], mine2, got2, both, us=1)
    kv2 = [half2, swap_y(half2, 3)]
    pair_out = [(stat, F32), (stat, F32), ((128, T), F32)]
    m1a, l1a, o1a = call(functools.partial(first_kernel, 0), pair_out, q_t, k, v_t, half2, us=2)
    all3, cot = call(pack3_kernel, [((256, F), BF), (wide, BF)], mine3, pair_a, pair_b, cotangent, m1a, us=1)
    kv3 = spread(all3, 1)
    cot_z = swap(cot, 2)
    cot_c = swap(cot, 1)
    cot_zc = swap(cot_z, 1)
    cots = [cot, cot_c, cot_z, cot_zc]
    m1b, l1b, o1b = call(functools.partial(first_kernel, 1), pair_out, q_t, k, v_t, all3, us=2)
    m2, l2, o2 = call(
        second_kernel, [(stat, F32), (stat, F32), ((F, 128), F32)], *kv2, q, us=6
    )
    (mine4,) = call(pack4_kernel, [((256, F), BF)], *kv3, m2, m1b, us=1)
    kv4 = spread(mine4, 16)
    m, l, o, g, g_t, lse, delta, att_part = call(
        third_kernel,
        [((8, 128), F32), ((8, 128), F32), ((F, 128), F32), (wide, BF), (tall, BF), (stat, F32), (stat, F32),
         (tall, F32)],
        pos, *kv3, q, m1a, l1a, o1a, m1b, l1b, o1b, m2, l2, o2, *cots, out_weight, mine4, us=8,
    )
    lse, delta, att, dq_first, *sent = call(
        fourth_kernel,
        [(stat, F32), (stat, F32), (tall, BF), ((F, 128), F32), ((512, F), F32)] + [((512, F), BF)] * 3,
        pos, *kv4, q, m, l, o, g, g_t, lse, delta, att_part, *cots, us=6,
        scratch=[pltpu.VMEM((4, T, F), BF)],
    )
    own2, sent2, dq_first = call(
        second_back_kernel, [((512, F), F32), ((512, F), BF), ((F, 128), F32)],
        *kv2, q, g, lse, delta, dq_first, us=2,
    )
    sent = lax.optimization_barrier((*sent, sent2))[:4]
    r4 = bring(sent, 16)
    got2 = swap_y(sent2, 3)
    send_c, keep_a, keep_b = call(
        project_kernel, [((2 * T, F), BF), (wide, F32), (wide, F32)], pos, att, out_weight, sent2, us=2
    )
    dk3, dv3, dq_first, dk_a, dv_a, dq_a = call(
        third_back_kernel,
        [(wide, F32), (wide, F32), ((F, 128), F32), ((T, 128), F32), ((T, 128), F32), ((128, T), F32)],
        *kv3, q, q_t, k, k_t, v, g, g_t, lse, delta, dq_first, us=6,
    )
    own2, sent2 = call(fold_kernel, [((256, F), F32), ((256, F), BF)], own2, got2, us=1)
    got2 = swap_y(sent2, 1)
    sent = call(
        reduce_y_kernel, [((320, F), F32)] + [((320, F), BF)] * 3, pos, *r4, dk3, dv3, got2, us=1,
        scratch=[pltpu.VMEM((512, F), F32)],
    )
    r3 = bring(sent, 1)
    got_c = swap(lax.optimization_barrier((send_c, sent[0]))[0], 1)
    mix_own, mix_send = call(mix_kernel, [(wide, F32), (wide, BF)], keep_a, keep_b, got_c, us=1)
    mix_got = swap(mix_send, 2)
    dk_b, dv_b, dq_b = call(
        pair_back_kernel, [((T, 128), F32), ((T, 128), F32), ((128, T), F32)],
        q, q_t, k, k_t, v, g, g_t, lse, delta, sent[1], us=6,
    )
    sent = call(
        reduce_z_kernel, [((80, F), F32)] + [((80, F), BF)] * 3, pos, *r3, us=1,
        scratch=[pltpu.VMEM((320, F), F32)],
    )
    rz = [sent[0]] + [swap_z(sent[n], n) for n in (1, 2, 3)]
    query_grad, dk_part, dv_part, dk_head, dv_head, mixed_out = call(
        natural_kernel, [(wide, BF), (wide, BF), (wide, BF), ((SEL3, F), F32), ((SEL3, F), F32), (wide, BF)],
        pos, dq_first, dk_a, dv_a, dq_a, dk_b, dv_b, dq_b, own2, got2, mix_own, mix_got, sent[1], us=6,
    )
    key_grad, value_grad, weight_grad = call(
        last_kernel, [(wide, BF), (wide, BF), ((16, F), F32)],
        pos, *rz, dk_head, dv_head, dk_part, dv_part, us=2,
    )
    return mixed_out, query_grad, key_grad, value_grad, weight_grad.T


def solution(mesh):
    rows = P("seq", "head")
    return jax.shard_map(
        body,
        mesh=mesh,
        in_specs=(rows, rows, rows, P("head", None), rows),
        out_specs=(rows, rows, rows, rows, P("head", "seq")),
        check_vma=False,
    )
```

```python
import functools

import functools

import jax
import jax.numpy as jnp
from jax import lax
from jax.experimental import pallas as pl
from jax.experimental.pallas import tpu as pltpu
from jax.sharding import PartitionSpec as P

HD = 64
NH = 4
T = 512
F = NH * HD
SEL2, SEL3, SEL4 = 128, 32, 8
SCALE = HD ** -0.5
NEG = -1e30
BF = jnp.bfloat16
F32 = jnp.float32


def iota(shape, dim):
    return lax.broadcasted_iota(jnp.int32, shape, dim)


def token_of(index):
    return (index >> 7) + ((index >> 5) & 3) * 4 + ((index >> 3) & 3) * 16 + (index & 7) * 64


def pick_mat(head, rows):
    wanted = (token_of(iota((rows, T), 0)) + head) & (T - 1)
    return jnp.where(wanted == iota((rows, T), 1), 1.0, 0.0).astype(BF)


def put_mat(head, cols):
    wanted = (token_of(iota((T, cols), 1)) + head) & (T - 1)
    return jnp.where(wanted == iota((T, cols), 0), 1.0, 0.0).astype(BF)


def dot(a, b, dims=((1,), (0,))):
    return lax.dot_general(a, b, (dims, ((), ())), preferred_element_type=F32)


def per_head_rows(mats, arrays):
    pairs = []
    for p in range(2):
        both = jnp.concatenate([a[:, 128 * p:128 * p + 128] for a in arrays], 1)
        even = dot(mats[2 * p], both)
        odd = dot(mats[2 * p + 1], both)
        pairs.append(jnp.where((iota(even.shape, 1) & 127) < HD, even, odd))
    return [
        jnp.concatenate([pair[:, 128 * n:128 * n + 128] for pair in pairs], 1)
        for n in range(len(arrays))
    ]


def head_blocks(rows, n):
    part = rows[:n]
    lane_head = iota(part.shape, 1) >> 6
    return jnp.concatenate([jnp.where(lane_head == h, part, 0.0) for h in range(NH)], 0)


def blocks_both(rows, n):
    full = head_blocks(rows, n)
    if NH * n < 128:
        full = jnp.concatenate([full, jnp.zeros((128 - NH * n, F), F32)], 0)
    return full.astype(BF), full.T.astype(BF)


def to_lanes(rows, n):
    total = None
    for h in range(NH):
        row = jnp.broadcast_to(jnp.where(iota((1, 128), 1) < n, rows[h], 0.0), (8, 128))
        if h:
            row = pltpu.roll(row, n * h, 1)
        total = row if total is None else total + row
    return total[0:1]


def from_lanes(rows, h, n, fill):
    if h:
        rows = pltpu.roll(rows, 128 - n * h, 1)
    return jnp.where(iota(rows.shape, 1) < n, rows, fill)


def soft(scores):
    peak = jnp.max(scores, axis=0, keepdims=True)
    weights = jnp.exp(scores - peak)
    return peak, jnp.sum(weights, axis=0, keepdims=True), weights.astype(BF)


def forward(keys, values, q_t):
    peak, total, weights = soft(dot(keys, q_t))
    return peak, total, dot(values, weights, ((0,), (0,)))


def backward(keys, values, q, q_t, g, g_t, lse, delta):
    prob = jnp.exp(dot(keys, q_t) - lse)
    ds = (prob * (dot(values, g_t) - delta)).astype(BF)
    d_values = dot(prob.astype(BF), g)
    d_keys = dot(ds, q)
    return d_keys, d_values, dot(keys, ds, ((0,), (0,)))


def diag_lanes(wide, n):
    return jnp.concatenate(
        [from_lanes(wide[HD * h:HD * h + HD], h, n, 0.0) for h in range(NH)], 0
    )


def half_mask(rows, h):
    return jnp.where((iota(rows.shape, 1) < HD) == (h % 2 == 0), rows.astype(F32), 0.0).astype(BF)


def half_pad(cols, h):
    zero = jnp.zeros_like(cols)
    return jnp.concatenate([cols, zero] if h % 2 == 0 else [zero, cols], 0)


def level1_backward(p, q_ref, q_t_ref, k_ref, k_t_ref, v_ref, g_ref, g_t_ref, lse_ref, delta_ref,
                    dk_ref, dv_ref, dq_ref):
    cols = slice(128 * p, 128 * p + 128)
    for h in (2 * p, 2 * p + 1):
        rows = slice(HD * h, HD * h + HD)
        for c in range(2):
            lanes = slice(256 * c, 256 * c + 256)
            q_t = half_pad(q_t_ref[rows, lanes], h)
            g_t = half_pad(g_t_ref[rows, lanes], h)
            prob = jnp.exp(dot(k_ref[:, cols], q_t) - lse_ref[h:h + 1, lanes])
            ds = (prob * (dot(v_ref[:, cols], g_t) - delta_ref[h:h + 1, lanes])).astype(BF)
            dv = dot(prob.astype(BF), half_mask(g_ref[lanes, cols], h))
            dk = dot(ds, half_mask(q_ref[lanes, cols], h))
            dq_ref[HD * (h % 2):HD * (h % 2) + HD, lanes] = dot(k_t_ref[rows, :], ds)
            if h % 2 == 0 and c == 0:
                dv_ref[...] = dv
                dk_ref[...] = dk
            else:
                dv_ref[...] += dv
                dk_ref[...] += dk


def blocks4(rows):
    full = jnp.concatenate([head_blocks(r.astype(F32), SEL4) for r in rows], 0)
    return full.astype(BF), full.T.astype(BF)


def fold_heads(wide):
    total = None
    for h in range(NH):
        part = wide[HD * h:HD * h + HD]
        part = jnp.where(((iota(part.shape, 1) >> 3) & 3) == h, part, 0.0)
        total = part if total is None else total + part
    return total


def first_lanes(rows, d):
    return pltpu.roll(rows, 128 - 32 * d, 1) if d else rows


def three(rows):
    high = rows.astype(BF)
    rest = rows - high.astype(F32)
    middle = rest.astype(BF)
    low = (rest - middle.astype(F32)).astype(BF)
    return [high.astype(F32), middle.astype(F32), low.astype(F32)]


def pick3_kernel(pos, k, v, out):
    mats = [pick_mat(pos[0] * NH + m, SEL3) for m in range(NH)]
    ks, vs = per_head_rows(mats, [k[...], v[...]])
    out[0:SEL3] = ks.astype(BF)
    out[SEL3:2 * SEL3] = vs.astype(BF)


def pick2_kernel(pos, k, v, _p3, out):
    mats = [pick_mat(pos[0] * NH + m, SEL2) for m in range(NH)]
    ks, vs = per_head_rows(mats, [k[...], v[...]])
    out[0:SEL2] = ks.astype(BF)
    out[SEL2:2 * SEL2] = vs.astype(BF)


def order_kernel(pos, q, k, v, _s, q_out, q_t_out, k_out, k_t_out, v_out, v_t_out, q4_out):
    mats = [pick_mat(pos[0] * NH + m, T) for m in range(NH)]
    qs, ks, vs = per_head_rows(mats, [q[...], k[...], v[...]])
    qs = qs * SCALE
    q_out[...] = qs.astype(BF)
    q4_out[...] = qs[0:16].astype(BF)
    q_t_out[...] = qs.T.astype(BF)
    k_out[...] = ks.astype(BF)
    k_t_out[...] = ks.T.astype(BF)
    v_out[...] = vs.astype(BF)
    v_t_out[...] = vs.T.astype(BF)


def first_kernel(p, q_t, k, v_t, _s, m_out, l_out, o_out):
    m_out[...] = jnp.zeros_like(m_out)
    l_out[...] = jnp.zeros_like(l_out)
    cols = slice(128 * p, 128 * p + 128)
    for h in range(2):
        rows_in = slice(HD * (2 * p + h), HD * (2 * p + h) + HD)
        rows = slice(HD * h, HD * h + HD)
        for c in range(2):
            lanes = slice(256 * c, 256 * c + 256)
            peak, total, weights = soft(dot(k[:, cols], half_pad(q_t[rows_in, lanes], h)))
            m_out[h:h + 1, lanes] = peak
            l_out[h:h + 1, lanes] = total
            o_out[rows, lanes] = dot(v_t[rows_in, :], weights)


def pair_kernel(a, b, _s, out):
    rows = a.shape[0]
    out[0:rows] = a[...]
    out[rows:2 * rows] = b[...]


def pack3_kernel(b, c, cot, _s, _t, out, cot_out):
    cot_out[...] = cot[...]
    for half in range(2):
        base = SEL3 * half
        for n, part in enumerate((b[base:base + SEL3], c[64 + base:64 + base + SEL3], c[base:base + SEL3])):
            out[96 * half + SEL3 * n:96 * half + SEL3 * n + SEL3] = part


def level2_places(a, b):
    return a.at[0:256], a.at[256:512], b.at[256:512], b.at[0:256]


def part4_kernel(a, b, c0, c1, c2, c3, qa, qb, _s, _t, out, part):
    for half in range(2):
        parts = []
        for here, others in zip(level2_places(a, b), (c0, c1, c2, c3)):
            parts.append(here[128 * half:128 * half + 16].astype(F32)[:SEL4])
            for n in range(3):
                start = 96 * half + SEL3 * n
                parts.append(others[start:start + 16].astype(F32)[:SEL4])
        out[128 * half:128 * half + 128] = jnp.concatenate(parts, 0).astype(BF)
    _, q_t = blocks4([qa[0:16], qa[16:32], qb[16:32], qb[0:16]])
    peak, total, weights = soft(dot(out[0:128], q_t))
    part[0:HD] = fold_heads(dot(out[128:256], weights, ((0,), (0,))))
    part[HD:HD + 8] = jnp.concatenate(
        [peak, total, jnp.zeros((6, 128), F32)], 0
    )


def stack_kv(refs):
    keys = jnp.concatenate([a[0:128] for a in refs], 0)
    values = jnp.concatenate([a[128:256] for a in refs], 0)
    return keys, values


def stack_kv3(a, b, others):
    keys, values = [], []
    for here, other in zip(level2_places(a, b), others):
        keys += [here[0:SEL3], other[0:96]]
        values += [here[128:128 + SEL3], other[96:192]]
    return jnp.concatenate(keys, 0), jnp.concatenate(values, 0)


def second_kernel(a, b, q, m_out, l_out, o_out):
    keys, values = stack_kv((a.at[0:256], a.at[256:512], b.at[0:256], b.at[256:512]))
    _, q_t = blocks_both(q[0:SEL2].astype(F32), SEL2)
    peak, total, wide = forward(keys, values, q_t)
    m_out[...] = jnp.broadcast_to(peak, m_out.shape)
    l_out[...] = jnp.broadcast_to(total, l_out.shape)
    o_out[...] = jnp.concatenate(
        [wide[HD * h:HD * h + HD, 128 * h:128 * h + 128] for h in range(NH)], 0
    )


def third_kernel(pos, a, b, a0, a1, a2, a3, q, m1a, l1a, o1a, m1b, l1b, o1b, m2, l2, o2, c0, c1, c2, c3, w, _p3,
                 m_out, l_out, o_out, g_out, g_t_out, lse_out, delta_out, att_out):
    here = pos[0]
    grad = None
    for r, c in enumerate((c0, c1, c2, c3)):
        at = pl.multiple_of((here ^ r) * F, F)
        term = dot(c[...], w[:, pl.ds(at, F)], ((1,), (1,)))
        grad = term if grad is None else grad + term
    mats = [pick_mat(here * NH + m, T) for m in range(NH)]
    (gs,) = per_head_rows(mats, [grad.astype(BF)])
    g_t = gs.T
    g_out[...] = gs.astype(BF)
    g_t_out[...] = g_t.astype(BF)

    keys, values = stack_kv3(a, b, (a0, a1, a2, a3))
    _, q_t = blocks_both(q[0:SEL3].astype(F32), SEL3)
    m3, l3, wide = forward(keys, values, q_t)
    m3 = jnp.broadcast_to(m3, (8, 128))
    l3 = jnp.broadcast_to(l3, (8, 128))
    lse_out[...] = jnp.zeros_like(lse_out)
    delta_out[...] = jnp.zeros_like(delta_out)
    m_out[...] = jnp.zeros_like(m_out)
    l_out[...] = jnp.zeros_like(l_out)
    for h in range(NH):
        rows = slice(HD * h, HD * h + HD)
        m1, l1, o1 = ((m1a, l1a, o1a), (m1b, l1b, o1b))[h // 2]
        one, half = slice(h % 2, h % 2 + 1), slice(HD * (h % 2), HD * (h % 2) + HD)
        ma, la, oa = m1[one, 0:128], l1[one, 0:128], o1[half, 0:128]
        mb, lb = m2[0:1, 128 * h:128 * h + 128], l2[0:1, 128 * h:128 * h + 128]
        mc = from_lanes(m3, h, SEL3, NEG)[0:1]
        lc = from_lanes(l3, h, SEL3, 0.0)[0:1]
        oc = from_lanes(wide[rows], h, SEL3, 0.0)
        top = jnp.maximum(jnp.maximum(ma, mb), mc)
        fa, fb, fc = jnp.exp(ma - top), jnp.exp(mb - top), jnp.exp(mc - top)
        m_out[h:h + 1] = top
        l_out[h:h + 1] = fa * la + fb * lb + fc * lc
        o_out[rows] = fa * oa + fb * o2[rows] + fc * oc
        total = l1[one, 128:T]
        out = o1[half, 128:T] / total
        lse_out[h:h + 1, 128:T] = m1[one, 128:T] + jnp.log(total)
        delta_out[h:h + 1, 128:T] = jnp.sum(g_t_out[rows, 128:T].astype(F32) * out, axis=0, keepdims=True)
        att_out[rows] = dot(out.astype(BF), mats[h][128:T])


def fourth_kernel(pos, r0, r1, r2, r3, m, l, o, g, g_t, lse_in, delta_in, att_in, c0, c1, c2, c3,
                  lse_out, delta_out, att_out, s0, s1, s2, s3, blocks):
    here, x_pos = pos[0], pos[1]
    parts = [first_lanes(r[...], d) for d, r in enumerate((r0, r1, r2, r3))]
    peaks = [r[HD:HD + 8] for r in parts]
    peak = jnp.maximum(jnp.maximum(peaks[0], peaks[1]), jnp.maximum(peaks[2], peaks[3]))[0:1]
    total, weighted = 0.0, 0.0
    for r in parts:
        factor = jnp.exp(r[HD:HD + 1] - peak)
        total = total + factor * r[HD + 1:HD + 2]
        weighted = weighted + factor * r[0:HD]
    peak = jnp.broadcast_to(peak, (8, 128))
    total = jnp.broadcast_to(total, (8, 128))
    lse_out[...] = lse_in[...]
    delta_out[...] = delta_in[...]
    lse_rows, delta_rows = [], []
    for h in range(NH):
        rows = slice(HD * h, HD * h + HD)
        ma, la, oa = m[h:h + 1], l[h:h + 1], o[rows]
        mb = from_lanes(peak, h, SEL4, NEG)[0:1]
        lb = from_lanes(total, h, SEL4, 0.0)[0:1]
        ob = from_lanes(weighted, h, SEL4, 0.0)
        top = jnp.maximum(ma, mb)
        fa, fb = jnp.exp(ma - top), jnp.exp(mb - top)
        denominator = fa * la + fb * lb
        out = (fa * oa + fb * ob) / denominator
        lse = top + jnp.log(denominator)
        delta = jnp.sum(g_t[rows, 0:128].astype(F32) * out, axis=0, keepdims=True)
        lse_out[h:h + 1, 0:128] = lse
        delta_out[h:h + 1, 0:128] = delta
        lse_rows.append(lse)
        delta_rows.append(delta)
        att = att_in[rows] + dot(out.astype(BF), pick_mat(here * NH + h, SEL2))
        att_out[rows] = att.astype(BF)
    stats = three(to_lanes(lse_rows, SEL4)) + three(to_lanes(delta_rows, SEL4)) + [jnp.zeros((2, 128), F32)]
    stats = jnp.concatenate(stats, 0)
    stats = jnp.concatenate([g[0:16].astype(F32)[0:SEL4], jnp.concatenate([stats, stats], 1)], 0).astype(BF)
    for r, c in enumerate((c0, c1, c2, c3)):
        blocks[here ^ r] = c[...]
    for d, s in enumerate((s0, s1, s2, s3)):
        term = dot(att_out[...], blocks[x_pos ^ d])
        s[0:256] = term.T.astype(s.dtype)
        s[256:272] = stats.astype(s.dtype)


def fourth_back_kernel(kv, qa, qb, b0, b1, b2, b3, d_keys, d_values, dq):
    q, q_t = blocks4([qa[0:16], qa[16:32], qb[16:32], qb[0:16]])
    news = [b[256:272].astype(F32) for b in (b0, b1, b2, b3)]
    g, g_t = blocks4(news)
    lse, delta = 0.0, 0.0
    for d, new in enumerate(news):
        for start in range(3):
            row_l = jnp.where(iota((1, 128), 1) < 32, new[8 + start:9 + start, 0:128], 0.0)
            row_d = jnp.where(iota((1, 128), 1) < 32, new[11 + start:12 + start, 0:128], 0.0)
            both = jnp.concatenate([row_l, row_d, jnp.zeros((6, 128), F32)], 0)
            both = pltpu.roll(both, 32 * d, 1) if d else both
            lse = lse + both[0:1]
            delta = delta + both[1:2]
    d_keys[...], d_values[...], wide = backward(kv[0:128], kv[128:256], q, q_t, g, g_t, lse, delta)
    dq[...] = fold_heads(wide)


def project_kernel(pos, att, w, _s, send, keep_a, keep_b):
    here = pos[0]
    for r, ref in ((0, keep_a), (2, keep_b), (1, send.at[0:T]), (3, send.at[T:2 * T])):
        at = pl.multiple_of((here ^ r) * F, F)
        ref[...] = dot(att[...], w[:, pl.ds(at, F)], ((0,), (0,))).astype(ref.dtype)


def second_back_kernel(a, b, q, g, lse, delta, own, send, dq_first):
    keys, values = stack_kv((a.at[0:256], a.at[256:512], b.at[0:256], b.at[256:512]))
    q2, q2_t = blocks_both(q[0:SEL2].astype(F32), SEL2)
    g2, g2_t = blocks_both(g[0:SEL2].astype(F32), SEL2)
    lse2 = jnp.concatenate([lse[h:h + 1, 0:128] for h in range(NH)], 1)
    delta2 = jnp.concatenate([delta[h:h + 1, 0:128] for h in range(NH)], 1)
    d_keys, d_values, wide = backward(keys, values, q2, q2_t, g2, g2_t, lse2, delta2)
    diag = [wide[HD * h:HD * h + HD, 128 * h:128 * h + 128] for h in range(NH)]
    dq_first[...] = jnp.concatenate(diag, 0)
    for n, (out, at) in enumerate(((own, 0), (own, 256), (send, 0), (send, 256))):
        out[at:at + 128] = d_keys[128 * n:128 * n + 128].astype(out.dtype)
        out[at + 128:at + 256] = d_values[128 * n:128 * n + 128].astype(out.dtype)


def fold_kernel(own, got, _s, keep, send):
    keep[...] = own[0:256] + got[0:256].astype(F32)
    send[...] = (own[256:512] + got[256:512].astype(F32)).astype(BF)


def third_back_kernel(a, b, a0, a1, a2, a3, q, q_t, k, k_t, v, g, g_t, lse, delta, dq_in,
                      dk3, dv3, dq_first, dk, dv, dq):
    keys, values = stack_kv3(a, b, (a0, a1, a2, a3))
    q3, q3_t = blocks_both(q[0:SEL3].astype(F32), SEL3)
    g3, g3_t = blocks_both(g[0:SEL3].astype(F32), SEL3)
    lse3 = to_lanes([lse[h:h + 1, 0:128] for h in range(NH)], SEL3)
    delta3 = to_lanes([delta[h:h + 1, 0:128] for h in range(NH)], SEL3)
    dk3[...], dv3[...], wide = backward(keys, values, q3, q3_t, g3, g3_t, lse3, delta3)
    dq_first[...] = dq_in[...] + diag_lanes(wide, SEL3)
    level1_backward(0, q, q_t, k, k_t, v, g, g_t, lse, delta, dk, dv, dq)


def pair_back_kernel(q, q_t, k, k_t, v, g, g_t, lse, delta, _s, dk, dv, dq):
    level1_backward(1, q, q_t, k, k_t, v, g, g_t, lse, delta, dk, dv, dq)


def reduce_y_kernel(pos, own, b1, b2, b3, dk4, dv4, dk3, dv3, _s, s0, s1, s2, s3, total):
    y_pos = pos[3]
    total[...] = own[0:256] + b1[0:256].astype(F32) + b2[0:256].astype(F32) + b3[0:256].astype(F32)
    for d, s in enumerate((s0, s1, s2, s3)):
        for base, level, fourth in ((0, dk3, dk4), (128, dv3, dv4)):
            parts = []
            for n in range(4):
                at = 128 * d + SEL3 * n
                start = SEL3 * d + SEL4 * n
                parts.append(level[at:at + SEL4] + fourth[start:start + SEL4])
                parts.append(level[at + SEL4:at + SEL3])
            s[base:base + 128] = jnp.concatenate(parts, 0).astype(s.dtype)
        for n in range(4):
            start = pl.multiple_of(64 * n + 16 * (y_pos ^ d), 16)
            s[256 + 16 * n:272 + 16 * n] = total[pl.ds(start, 16)].astype(s.dtype)


def reduce_z_kernel(pos, own, b1, b2, b3, s0, s1, s2, s3, total):
    z_pos = pos[2]
    total[...] = own[...] + b1[...].astype(F32) + b2[...].astype(F32) + b3[...].astype(F32)
    for d, s in enumerate((s0, s1, s2, s3)):
        s[0:SEL3] = total[SEL3 * d:SEL3 * d + SEL3].astype(s.dtype)
        s[SEL3:2 * SEL3] = total[128 + SEL3 * d:128 + SEL3 * d + SEL3].astype(s.dtype)
        start = pl.multiple_of(256 + 16 * (z_pos ^ d), 16)
        s[64:80] = total[pl.ds(start, 16)].astype(s.dtype)


def fold4_kernel(own, got, keep, send):
    keep[...] = own[...] + first_lanes(got[...], 3)
    send[...] = first_lanes(own[...], 1) + first_lanes(got[...], 2)


def mix_kernel(keep_a, keep_b, got, own, send):
    own[...] = keep_a[...] + got[0:T].astype(F32)
    send[...] = (keep_b[...] + got[T:2 * T].astype(F32)).astype(BF)


def natural_kernel(pos, e0, e1, dq_first, dk_a, dv_a, dq_a, dk_b, dv_b, dq_b, own2, got2, mix_own, mix_got, _s,
                   dq_out, dk_part, dv_part, dk_head, dv_head, mixed_out):
    mixed_out[...] = (mix_own[...] + mix_got[...].astype(F32)).astype(BF)
    level2 = own2[...] + got2[...].astype(F32)
    dq4 = e0[...] + e1[...]
    for p, (dk, dv, dq) in enumerate(((dk_a, dv_a, dq_a), (dk_b, dv_b, dq_b))):
        cols = slice(128 * p, 128 * p + 128)
        dk_top = dk[0:SEL2] + level2[0:SEL2, cols]
        dv_top = dv[0:SEL2] + level2[SEL2:2 * SEL2, cols]
        dk_head[:, cols] = dk_top[0:SEL3]
        dv_head[:, cols] = dv_top[0:SEL3]
        dq4_pair = jnp.concatenate([from_lanes(dq4, h, SEL4, 0.0) for h in (2 * p, 2 * p + 1)], 0)
        dq_t = jnp.concatenate([dq[:, 0:128] + dq_first[cols] + dq4_pair, dq[:, 128:T]], 1) * SCALE
        later = [
            jnp.concatenate([jnp.zeros((SEL3, 128), F32), top[SEL3:SEL2], rest[SEL2:T]], 0)
            for top, rest in ((dk_top, dk), (dv_top, dv))
        ]
        both = jnp.concatenate(later + [dq_t.T], 1).astype(BF)
        even = dot(put_mat(pos[0] * NH + 2 * p, T), both)
        odd = dot(put_mat(pos[0] * NH + 2 * p + 1, T), both)
        natural = jnp.where((iota(even.shape, 1) & 127) < HD, even, odd)
        dk_part[:, cols] = natural[:, 0:128].astype(BF)
        dv_part[:, cols] = natural[:, 128:256].astype(BF)
        dq_out[:, cols] = natural[:, 256:384].astype(BF)


def last_kernel(pos, own, b1, b2, b3, dk_head, dv_head, dk_part, dv_part, dk_out, dv_out, w_out):
    total = own[...] + b1[...].astype(F32) + b2[...].astype(F32) + b3[...].astype(F32)
    ks = (total[0:SEL3] + dk_head[...]).astype(BF)
    vs = (total[SEL3:2 * SEL3] + dv_head[...]).astype(BF)
    w_out[...] = total[64:80]
    mats = [put_mat(pos[0] * NH + m, SEL3) for m in range(NH)]
    ks, vs = per_head_rows(mats, [ks, vs])
    dk_out[...] = (ks + dk_part[...].astype(F32)).astype(BF)
    dv_out[...] = (vs + dv_part[...].astype(F32)).astype(BF)


def call(kernel, outs, *args, us=5, scratch=()):
    def spec(arg):
        return pl.BlockSpec(memory_space=pltpu.SMEM if arg.dtype == jnp.int32 else pltpu.VMEM)

    return pl.pallas_call(
        kernel,
        out_shape=[jax.ShapeDtypeStruct(shape, dtype) for shape, dtype in outs],
        in_specs=[spec(a) for a in args],
        out_specs=[pl.BlockSpec(memory_space=pltpu.VMEM)] * len(outs),
        scratch_shapes=scratch,
        compiler_params=pltpu.CompilerParams(vmem_limit_bytes=24 * 2 ** 20),
        cost_estimate=pl.CostEstimate(flops=us * 500_000_000, bytes_accessed=us * 1_000_000, transcendentals=0),
        name=getattr(kernel, "func", kernel).__name__,
    )(*args)


def swap_x(block, mask):
    return lax.ppermute(block, "seq", [(s, s ^ (16 * mask)) for s in range(64)])


def swap_z(block, mask):
    return lax.ppermute(block, "seq", [(s, s ^ (4 * mask)) for s in range(64)])


def swap_y(block, mask):
    return lax.ppermute(block, "seq", [(s, s ^ mask) for s in range(64)])


def swap(block, mask):
    return lax.ppermute(block, "head", [(s, s ^ mask) for s in range(4)])


def body(query_act, key_act, value_act, out_weight, cotangent):
    seq = lax.axis_index("seq")
    head = lax.axis_index("head")
    pos = jnp.stack([head, seq // 16, seq // 4 % 4, seq % 4]).astype(jnp.int32)
    wide, tall, stat = (T, F), (F, T), (8, T)

    (mine3,) = call(pick3_kernel, [((64, F), BF)], pos, key_act, value_act, us=1)
    pair_a = swap_z(mine3, 1)
    (mine2,) = call(pick2_kernel, [((256, F), BF)], pos, key_act, value_act, mine3, us=1)
    got2 = swap_y(mine2, 1)
    q, q_t, k, k_t, v, v_t, q4 = call(
        order_kernel, [(wide, BF), (tall, BF)] * 3 + [((16, F), BF)], pos, query_act, key_act, value_act, mine2, us=3,
    )
    (both,) = call(pair_kernel, [((128, F), BF)], mine3, pair_a, q, us=1)
    pair_b = swap_z(both, 3)
    (half2,) = call(pair_kernel, [((512, F), BF)], mine2, got2, both, us=1)
    kv2 = [half2, swap_y(half2, 3)]
    (q4_both,) = call(pair_kernel, [((32, F), BF)], q4, swap_x(q4, 1), both, us=1)
    q4 = [q4_both, swap_x(q4_both, 3)]
    pair_out = [(stat, F32), (stat, F32), ((128, T), F32)]
    m1a, l1a, o1a = call(functools.partial(first_kernel, 0), pair_out, q_t, k, v_t, half2, us=2)
    all3, cot = call(pack3_kernel, [((192, F), BF), (wide, BF)], pair_a, pair_b, cotangent, m1a, q4[1], us=1)
    kv3 = [*kv2, all3] + [swap_y(all3, n) for n in (1, 2, 3)]
    cot_z = swap(cot, 2)
    cot_c = swap(cot, 1)
    cot_zc = swap(cot_z, 1)
    cots = [cot, cot_c, cot_z, cot_zc]
    m1b, l1b, o1b = call(functools.partial(first_kernel, 1), pair_out, q_t, k, v_t, all3, us=2)
    m2, l2, o2 = call(
        second_kernel, [(stat, F32), (stat, F32), ((F, 128), F32)], *kv2, q, us=6
    )
    kv4, mine4 = call(part4_kernel, [((256, F), BF), ((HD + 8, 128), F32)], *kv3, *q4, m2, m1b, us=1)
    parts = [mine4] + [swap_x(mine4, n) for n in (1, 2, 3)]
    m, l, o, g, g_t, lse, delta, att_part = call(
        third_kernel,
        [((8, 128), F32), ((8, 128), F32), ((F, 128), F32), (wide, BF), (tall, BF), (stat, F32), (stat, F32),
         (tall, F32)],
        pos, *kv3, q, m1a, l1a, o1a, m1b, l1b, o1b, m2, l2, o2, *cots, out_weight, mine4, us=8,
    )
    lse, delta, att, *sent = call(
        fourth_kernel,
        [(stat, F32), (stat, F32), (tall, BF), ((272, F), F32)] + [((272, F), BF)] * 3,
        pos, *parts, m, l, o, g, g_t, lse, delta, att_part, *cots, us=6,
        scratch=[pltpu.VMEM((4, T, F), BF)],
    )
    own2, sent2, dq_first = call(
        second_back_kernel, [((512, F), F32), ((512, F), BF), ((F, 128), F32)],
        *kv2, q, g, lse, delta, us=2,
    )
    r4 = [sent[0]] + [swap_x(sent[n], n) for n in (1, 2, 3)]
    got2 = swap_y(sent2, 3)
    send_c, keep_a, keep_b = call(
        project_kernel, [((2 * T, F), BF), (wide, F32), (wide, F32)], pos, att, out_weight, sent2, us=2
    )
    dk3, dv3, dq_first, dk_a, dv_a, dq_a = call(
        third_back_kernel,
        [(wide, F32), (wide, F32), ((F, 128), F32), ((T, 128), F32), ((T, 128), F32), ((128, T), F32)],
        *kv3, q, q_t, k, k_t, v, g, g_t, lse, delta, dq_first, us=6,
    )
    own2, sent2 = call(fold_kernel, [((256, F), F32), ((256, F), BF)], own2, got2, r4[3], us=1)
    got2 = swap_y(sent2, 1)
    dk4, dv4, dq4 = call(
        fourth_back_kernel, [((128, F), F32), ((128, F), F32), ((HD, 128), F32)], kv4, *q4, *r4, us=1,
    )
    sent = call(
        reduce_y_kernel, [((320, F), F32)] + [((320, F), BF)] * 3, pos, *r4, dk4, dv4, dk3, dv3, sent2, us=1,
        scratch=[pltpu.VMEM((256, F), F32)],
    )
    got4 = swap_x(lax.optimization_barrier((dq4, sent[0]))[0], 3)
    dq4, dq4_send = call(fold4_kernel, [((HD, 128), F32)] * 2, dq4, got4, us=1)
    got4 = swap_x(dq4_send, 1)
    r3 = [sent[0]] + [swap_y(sent[n], n) for n in (1, 2, 3)]
    got_c = swap(lax.optimization_barrier((send_c, sent[0]))[0], 1)
    mix_own, mix_send = call(mix_kernel, [(wide, F32), (wide, BF)], keep_a, keep_b, got_c, us=1)
    mix_got = swap(mix_send, 2)
    dk_b, dv_b, dq_b = call(
        pair_back_kernel, [((T, 128), F32), ((T, 128), F32), ((128, T), F32)],
        q, q_t, k, k_t, v, g, g_t, lse, delta, sent[1], us=6,
    )
    sent = call(
        reduce_z_kernel, [((80, F), F32)] + [((80, F), BF)] * 3, pos, *r3, us=1,
        scratch=[pltpu.VMEM((320, F), F32)],
    )
    rz = [sent[0]] + [swap_z(sent[n], n) for n in (1, 2, 3)]
    query_grad, dk_part, dv_part, dk_head, dv_head, mixed_out = call(
        natural_kernel, [(wide, BF), (wide, BF), (wide, BF), ((SEL3, F), F32), ((SEL3, F), F32), (wide, BF)],
        pos, dq4, got4, dq_first, dk_a, dv_a, dq_a, dk_b, dv_b, dq_b, own2, got2, mix_own, mix_got, sent[1], us=6,
    )
    key_grad, value_grad, weight_grad = call(
        last_kernel, [(wide, BF), (wide, BF), ((16, F), F32)],
        pos, *rz, dk_head, dv_head, dk_part, dv_part, us=2,
    )
    return mixed_out, query_grad, key_grad, value_grad, weight_grad.T


def solution(mesh):
    rows = P("seq", "head")
    return jax.shard_map(
        body,
        mesh=mesh,
        in_specs=(rows, rows, rows, P("head", None), rows),
        out_specs=(rows, rows, rows, rows, P("head", "seq")),
        check_vma=False,
    )
```

```python
import functools

import functools

import jax
import jax.numpy as jnp
from jax import lax
from jax.experimental import pallas as pl
from jax.experimental.pallas import tpu as pltpu
from jax.sharding import PartitionSpec as P

HD = 64
NH = 4
T = 512
F = NH * HD
SEL2, SEL3, SEL4 = 128, 32, 8
SCALE = HD ** -0.5
NEG = -1e30
BF = jnp.bfloat16
F32 = jnp.float32


def iota(shape, dim):
    return lax.broadcasted_iota(jnp.int32, shape, dim)


def token_of(index):
    return (index >> 7) + ((index >> 5) & 3) * 4 + ((index >> 3) & 3) * 16 + (index & 7) * 64


def pick_mat(head, rows):
    wanted = (token_of(iota((rows, T), 0)) + head) & (T - 1)
    return jnp.where(wanted == iota((rows, T), 1), 1.0, 0.0).astype(BF)


def put_mat(head, cols):
    wanted = (token_of(iota((T, cols), 1)) + head) & (T - 1)
    return jnp.where(wanted == iota((T, cols), 0), 1.0, 0.0).astype(BF)


def dot(a, b, dims=((1,), (0,))):
    return lax.dot_general(a, b, (dims, ((), ())), preferred_element_type=F32)


def per_head_rows(mats, arrays):
    pairs = []
    for p in range(2):
        both = jnp.concatenate([a[:, 128 * p:128 * p + 128] for a in arrays], 1)
        even = dot(mats[2 * p], both)
        odd = dot(mats[2 * p + 1], both)
        pairs.append(jnp.where((iota(even.shape, 1) & 127) < HD, even, odd))
    return [
        jnp.concatenate([pair[:, 128 * n:128 * n + 128] for pair in pairs], 1)
        for n in range(len(arrays))
    ]


def head_blocks(rows, n):
    part = rows[:n]
    lane_head = iota(part.shape, 1) >> 6
    return jnp.concatenate([jnp.where(lane_head == h, part, 0.0) for h in range(NH)], 0)


def blocks_both(rows, n):
    full = head_blocks(rows, n)
    if NH * n < 128:
        full = jnp.concatenate([full, jnp.zeros((128 - NH * n, F), F32)], 0)
    return full.astype(BF), full.T.astype(BF)


def to_lanes(rows, n):
    total = None
    for h in range(NH):
        row = jnp.broadcast_to(jnp.where(iota((1, 128), 1) < n, rows[h], 0.0), (8, 128))
        if h:
            row = pltpu.roll(row, n * h, 1)
        total = row if total is None else total + row
    return total[0:1]


def from_lanes(rows, h, n, fill):
    if h:
        rows = pltpu.roll(rows, 128 - n * h, 1)
    return jnp.where(iota(rows.shape, 1) < n, rows, fill)


def soft(scores):
    peak = jnp.max(scores, axis=0, keepdims=True)
    weights = jnp.exp(scores - peak)
    return peak, jnp.sum(weights, axis=0, keepdims=True), weights.astype(BF)


def forward(keys, values, q_t):
    peak, total, weights = soft(dot(keys, q_t))
    return peak, total, dot(values, weights, ((0,), (0,)))


def backward(keys, values, q, q_t, g, g_t, lse, delta):
    prob = jnp.exp(dot(keys, q_t) - lse)
    ds = (prob * (dot(values, g_t) - delta)).astype(BF)
    d_values = dot(prob.astype(BF), g)
    d_keys = dot(ds, q)
    return d_keys, d_values, dot(keys, ds, ((0,), (0,)))


def diag_lanes(wide, n):
    return jnp.concatenate(
        [from_lanes(wide[HD * h:HD * h + HD], h, n, 0.0) for h in range(NH)], 0
    )


def half_mask(rows, h):
    return jnp.where((iota(rows.shape, 1) < HD) == (h % 2 == 0), rows.astype(F32), 0.0).astype(BF)


def half_pad(cols, h):
    zero = jnp.zeros_like(cols)
    return jnp.concatenate([cols, zero] if h % 2 == 0 else [zero, cols], 0)


def level1_backward(p, q_ref, q_t_ref, k_ref, k_t_ref, v_ref, g_ref, g_t_ref, lse_ref, delta_ref,
                    dk_ref, dv_ref, dq_ref):
    cols = slice(128 * p, 128 * p + 128)
    for h in (2 * p, 2 * p + 1):
        rows = slice(HD * h, HD * h + HD)
        for c in range(2):
            lanes = slice(256 * c, 256 * c + 256)
            q_t = half_pad(q_t_ref[rows, lanes], h)
            g_t = half_pad(g_t_ref[rows, lanes], h)
            prob = jnp.exp(dot(k_ref[:, cols], q_t) - lse_ref[h:h + 1, lanes])
            ds = (prob * (dot(v_ref[:, cols], g_t) - delta_ref[h:h + 1, lanes])).astype(BF)
            dv = dot(prob.astype(BF), half_mask(g_ref[lanes, cols], h))
            dk = dot(ds, half_mask(q_ref[lanes, cols], h))
            dq_ref[HD * (h % 2):HD * (h % 2) + HD, lanes] = dot(k_t_ref[rows, :], ds)
            if h % 2 == 0 and c == 0:
                dv_ref[...] = dv
                dk_ref[...] = dk
            else:
                dv_ref[...] += dv
                dk_ref[...] += dk


def blocks4(rows):
    full = jnp.concatenate([head_blocks(r.astype(F32), SEL4) for r in rows], 0)
    return full.astype(BF), full.T.astype(BF)


def fold_heads(wide):
    total = None
    for h in range(NH):
        part = wide[HD * h:HD * h + HD]
        part = jnp.where(((iota(part.shape, 1) >> 3) & 3) == h, part, 0.0)
        total = part if total is None else total + part
    return total


def first_lanes(rows, d):
    return pltpu.roll(rows, 128 - 32 * d, 1) if d else rows


def three(rows):
    high = rows.astype(BF)
    rest = rows - high.astype(F32)
    middle = rest.astype(BF)
    low = (rest - middle.astype(F32)).astype(BF)
    return [high.astype(F32), middle.astype(F32), low.astype(F32)]


def pick3_kernel(pos, k, v, out):
    mats = [pick_mat(pos[0] * NH + m, SEL3) for m in range(NH)]
    ks, vs = per_head_rows(mats, [k[...], v[...]])
    out[0:SEL3] = ks.astype(BF)
    out[SEL3:2 * SEL3] = vs.astype(BF)


def pick2_kernel(pos, k, v, _p3, out):
    mats = [pick_mat(pos[0] * NH + m, SEL2) for m in range(NH)]
    ks, vs = per_head_rows(mats, [k[...], v[...]])
    out[0:SEL2] = ks.astype(BF)
    out[SEL2:2 * SEL2] = vs.astype(BF)


def order_kernel(pos, q, k, v, _s, q_out, q_t_out, k_out, k_t_out, v_out, v_t_out, q4_out):
    mats = [pick_mat(pos[0] * NH + m, T) for m in range(NH)]
    qs, ks, vs = per_head_rows(mats, [q[...], k[...], v[...]])
    qs = qs * SCALE
    q_out[...] = qs.astype(BF)
    q4_out[...] = qs[0:16].astype(BF)
    q_t_out[...] = qs.T.astype(BF)
    k_out[...] = ks.astype(BF)
    k_t_out[...] = ks.T.astype(BF)
    v_out[...] = vs.astype(BF)
    v_t_out[...] = vs.T.astype(BF)


def first_kernel(p, q_t, k, v_t, _s, m_out, l_out, o_out):
    m_out[...] = jnp.zeros_like(m_out)
    l_out[...] = jnp.zeros_like(l_out)
    cols = slice(128 * p, 128 * p + 128)
    for h in range(2):
        rows_in = slice(HD * (2 * p + h), HD * (2 * p + h) + HD)
        rows = slice(HD * h, HD * h + HD)
        for c in range(2):
            lanes = slice(256 * c, 256 * c + 256)
            peak, total, weights = soft(dot(k[:, cols], half_pad(q_t[rows_in, lanes], h)))
            m_out[h:h + 1, lanes] = peak
            l_out[h:h + 1, lanes] = total
            o_out[rows, lanes] = dot(v_t[rows_in, :], weights)


def pair_kernel(a, b, _s, out):
    rows = a.shape[0]
    out[0:rows] = a[...]
    out[rows:2 * rows] = b[...]


def pack3_kernel(b, c, cot, _s, _t, out, cot_out):
    cot_out[...] = cot[...]
    for half in range(2):
        base = SEL3 * half
        for n, part in enumerate((b[base:base + SEL3], c[64 + base:64 + base + SEL3], c[base:base + SEL3])):
            out[96 * half + SEL3 * n:96 * half + SEL3 * n + SEL3] = part


def level2_places(a, b):
    return a.at[0:256], a.at[256:512], b.at[256:512], b.at[0:256]


def part4_kernel(a, b, c0, c1, c2, c3, qa, qb, _s, _t, out, part):
    for half in range(2):
        parts = []
        for here, others in zip(level2_places(a, b), (c0, c1, c2, c3)):
            parts.append(here[128 * half:128 * half + 16].astype(F32)[:SEL4])
            for n in range(3):
                start = 96 * half + SEL3 * n
                parts.append(others[start:start + 16].astype(F32)[:SEL4])
        out[128 * half:128 * half + 128] = jnp.concatenate(parts, 0).astype(BF)
    _, q_t = blocks4([qa[0:16], qa[16:32], qb[16:32], qb[0:16]])
    peak, total, weights = soft(dot(out[0:128], q_t))
    part[0:HD] = fold_heads(dot(out[128:256], weights, ((0,), (0,))))
    part[HD:HD + 8] = jnp.concatenate(
        [peak, total, jnp.zeros((6, 128), F32)], 0
    )


def stack_kv(refs):
    keys = jnp.concatenate([a[0:128] for a in refs], 0)
    values = jnp.concatenate([a[128:256] for a in refs], 0)
    return keys, values


def stack_kv3(a, b, others):
    keys, values = [], []
    for here, other in zip(level2_places(a, b), others):
        keys += [here[0:SEL3], other[0:96]]
        values += [here[128:128 + SEL3], other[96:192]]
    return jnp.concatenate(keys, 0), jnp.concatenate(values, 0)


def second_kernel(a, b, q, m_out, l_out, o_out):
    keys, values = stack_kv((a.at[0:256], a.at[256:512], b.at[0:256], b.at[256:512]))
    _, q_t = blocks_both(q[0:SEL2].astype(F32), SEL2)
    peak, total, wide = forward(keys, values, q_t)
    m_out[...] = jnp.broadcast_to(peak, m_out.shape)
    l_out[...] = jnp.broadcast_to(total, l_out.shape)
    o_out[...] = jnp.concatenate(
        [wide[HD * h:HD * h + HD, 128 * h:128 * h + 128] for h in range(NH)], 0
    )


def third_kernel(pos, a, b, a0, a1, a2, a3, q, m1a, l1a, o1a, m1b, l1b, o1b, m2, l2, o2, c0, c1, c2, c3, w, _p3,
                 m_out, l_out, o_out, g_out, g_t_out, lse_out, delta_out, att_out):
    here = pos[0]
    grad = None
    for r, c in enumerate((c0, c1, c2, c3)):
        at = pl.multiple_of((here ^ r) * F, F)
        term = dot(c[...], w[:, pl.ds(at, F)], ((1,), (1,)))
        grad = term if grad is None else grad + term
    mats = [pick_mat(here * NH + m, T) for m in range(NH)]
    (gs,) = per_head_rows(mats, [grad.astype(BF)])
    g_t = gs.T
    g_out[...] = gs.astype(BF)
    g_t_out[...] = g_t.astype(BF)

    keys, values = stack_kv3(a, b, (a0, a1, a2, a3))
    _, q_t = blocks_both(q[0:SEL3].astype(F32), SEL3)
    m3, l3, wide = forward(keys, values, q_t)
    m3 = jnp.broadcast_to(m3, (8, 128))
    l3 = jnp.broadcast_to(l3, (8, 128))
    lse_out[...] = jnp.zeros_like(lse_out)
    delta_out[...] = jnp.zeros_like(delta_out)
    m_out[...] = jnp.zeros_like(m_out)
    l_out[...] = jnp.zeros_like(l_out)
    for h in range(NH):
        rows = slice(HD * h, HD * h + HD)
        m1, l1, o1 = ((m1a, l1a, o1a), (m1b, l1b, o1b))[h // 2]
        one, half = slice(h % 2, h % 2 + 1), slice(HD * (h % 2), HD * (h % 2) + HD)
        ma, la, oa = m1[one, 0:128], l1[one, 0:128], o1[half, 0:128]
        mb, lb = m2[0:1, 128 * h:128 * h + 128], l2[0:1, 128 * h:128 * h + 128]
        mc = from_lanes(m3, h, SEL3, NEG)[0:1]
        lc = from_lanes(l3, h, SEL3, 0.0)[0:1]
        oc = from_lanes(wide[rows], h, SEL3, 0.0)
        top = jnp.maximum(jnp.maximum(ma, mb), mc)
        fa, fb, fc = jnp.exp(ma - top), jnp.exp(mb - top), jnp.exp(mc - top)
        m_out[h:h + 1] = top
        l_out[h:h + 1] = fa * la + fb * lb + fc * lc
        o_out[rows] = fa * oa + fb * o2[rows] + fc * oc
        total = l1[one, 128:T]
        out = o1[half, 128:T] / total
        lse_out[h:h + 1, 128:T] = m1[one, 128:T] + jnp.log(total)
        delta_out[h:h + 1, 128:T] = jnp.sum(g_t_out[rows, 128:T].astype(F32) * out, axis=0, keepdims=True)
        att_out[rows] = dot(out.astype(BF), mats[h][128:T])


def fourth_kernel(pos, r0, r1, r2, r3, m, l, o, g, g_t, lse_in, delta_in, att_in, c0, c1, c2, c3,
                  lse_out, delta_out, att_out, s0, s1, s2, s3, blocks):
    here, x_pos = pos[0], pos[1]
    parts = [first_lanes(r[...], d) for d, r in enumerate((r0, r1, r2, r3))]
    peaks = [r[HD:HD + 8] for r in parts]
    peak = jnp.maximum(jnp.maximum(peaks[0], peaks[1]), jnp.maximum(peaks[2], peaks[3]))[0:1]
    total, weighted = 0.0, 0.0
    for r in parts:
        factor = jnp.exp(r[HD:HD + 1] - peak)
        total = total + factor * r[HD + 1:HD + 2]
        weighted = weighted + factor * r[0:HD]
    peak = jnp.broadcast_to(peak, (8, 128))
    total = jnp.broadcast_to(total, (8, 128))
    lse_out[...] = lse_in[...]
    delta_out[...] = delta_in[...]
    lse_rows, delta_rows = [], []
    for h in range(NH):
        rows = slice(HD * h, HD * h + HD)
        ma, la, oa = m[h:h + 1], l[h:h + 1], o[rows]
        mb = from_lanes(peak, h, SEL4, NEG)[0:1]
        lb = from_lanes(total, h, SEL4, 0.0)[0:1]
        ob = from_lanes(weighted, h, SEL4, 0.0)
        top = jnp.maximum(ma, mb)
        fa, fb = jnp.exp(ma - top), jnp.exp(mb - top)
        denominator = fa * la + fb * lb
        out = (fa * oa + fb * ob) / denominator
        lse = top + jnp.log(denominator)
        delta = jnp.sum(g_t[rows, 0:128].astype(F32) * out, axis=0, keepdims=True)
        lse_out[h:h + 1, 0:128] = lse
        delta_out[h:h + 1, 0:128] = delta
        lse_rows.append(lse)
        delta_rows.append(delta)
        att = att_in[rows] + dot(out.astype(BF), pick_mat(here * NH + h, SEL2))
        att_out[rows] = att.astype(BF)
    stats = three(to_lanes(lse_rows, SEL4)) + three(to_lanes(delta_rows, SEL4)) + [jnp.zeros((2, 128), F32)]
    stats = jnp.concatenate(stats, 0)
    stats = jnp.concatenate([g[0:16].astype(F32)[0:SEL4], jnp.concatenate([stats, stats], 1)], 0).astype(BF)
    for r, c in enumerate((c0, c1, c2, c3)):
        blocks[here ^ r] = c[...]
    for d, s in enumerate((s0, s1, s2, s3)):
        term = dot(att_out[...], blocks[x_pos ^ d])
        s[0:256] = term.T.astype(s.dtype)
        s[256:272] = stats.astype(s.dtype)


def fourth_back_kernel(kv, qa, qb, b0, b1, b2, b3, d_keys, d_values, dq):
    q, q_t = blocks4([qa[0:16], qa[16:32], qb[16:32], qb[0:16]])
    news = [b[256:272].astype(F32) for b in (b0, b1, b2, b3)]
    g, g_t = blocks4(news)
    lse, delta = 0.0, 0.0
    for d, new in enumerate(news):
        for start in range(3):
            row_l = jnp.where(iota((1, 128), 1) < 32, new[8 + start:9 + start, 0:128], 0.0)
            row_d = jnp.where(iota((1, 128), 1) < 32, new[11 + start:12 + start, 0:128], 0.0)
            both = jnp.concatenate([row_l, row_d, jnp.zeros((6, 128), F32)], 0)
            both = pltpu.roll(both, 32 * d, 1) if d else both
            lse = lse + both[0:1]
            delta = delta + both[1:2]
    d_keys[...], d_values[...], wide = backward(kv[0:128], kv[128:256], q, q_t, g, g_t, lse, delta)
    dq[...] = fold_heads(wide)


def project_kernel(pos, att, w, _s, send, keep_a, keep_b):
    here = pos[0]
    for r, ref in ((0, keep_a), (2, keep_b), (1, send.at[0:T]), (3, send.at[T:2 * T])):
        at = pl.multiple_of((here ^ r) * F, F)
        ref[...] = dot(att[...], w[:, pl.ds(at, F)], ((0,), (0,))).astype(ref.dtype)


def second_back_kernel(a, b, q, g, lse, delta, own, send, dq_first):
    keys, values = stack_kv((a.at[0:256], a.at[256:512], b.at[0:256], b.at[256:512]))
    q2, q2_t = blocks_both(q[0:SEL2].astype(F32), SEL2)
    g2, g2_t = blocks_both(g[0:SEL2].astype(F32), SEL2)
    lse2 = jnp.concatenate([lse[h:h + 1, 0:128] for h in range(NH)], 1)
    delta2 = jnp.concatenate([delta[h:h + 1, 0:128] for h in range(NH)], 1)
    d_keys, d_values, wide = backward(keys, values, q2, q2_t, g2, g2_t, lse2, delta2)
    diag = [wide[HD * h:HD * h + HD, 128 * h:128 * h + 128] for h in range(NH)]
    dq_first[...] = jnp.concatenate(diag, 0)
    for n, (out, at) in enumerate(((own, 0), (own, 256), (send, 0), (send, 256))):
        out[at:at + 128] = d_keys[128 * n:128 * n + 128].astype(out.dtype)
        out[at + 128:at + 256] = d_values[128 * n:128 * n + 128].astype(out.dtype)


def fold_kernel(own, got, _s, keep, send):
    keep[...] = own[0:256] + got[0:256].astype(F32)
    send[...] = (own[256:512] + got[256:512].astype(F32)).astype(BF)


def third_back_kernel(a, b, a0, a1, a2, a3, q, q_t, k, k_t, v, g, g_t, lse, delta, dq_in,
                      dk3, dv3, dq_first, dk, dv, dq):
    keys, values = stack_kv3(a, b, (a0, a1, a2, a3))
    q3, q3_t = blocks_both(q[0:SEL3].astype(F32), SEL3)
    g3, g3_t = blocks_both(g[0:SEL3].astype(F32), SEL3)
    lse3 = to_lanes([lse[h:h + 1, 0:128] for h in range(NH)], SEL3)
    delta3 = to_lanes([delta[h:h + 1, 0:128] for h in range(NH)], SEL3)
    dk3[...], dv3[...], wide = backward(keys, values, q3, q3_t, g3, g3_t, lse3, delta3)
    dq_first[...] = dq_in[...] + diag_lanes(wide, SEL3)
    level1_backward(0, q, q_t, k, k_t, v, g, g_t, lse, delta, dk, dv, dq)


def pair_back_kernel(q, q_t, k, k_t, v, g, g_t, lse, delta, _s, dk, dv, dq):
    level1_backward(1, q, q_t, k, k_t, v, g, g_t, lse, delta, dk, dv, dq)


def reduce_y_kernel(pos, own, b1, b2, b3, dk4, dv4, dk3, dv3, _s, s0, s1, s2, s3, total):
    y_pos = pos[3]
    total[...] = own[0:256] + b1[0:256].astype(F32) + b2[0:256].astype(F32) + b3[0:256].astype(F32)
    for d, s in enumerate((s0, s1, s2, s3)):
        for base, level, fourth in ((0, dk3, dk4), (128, dv3, dv4)):
            parts = []
            for n in range(4):
                at = 128 * d + SEL3 * n
                start = SEL3 * d + SEL4 * n
                parts.append(level[at:at + SEL4] + fourth[start:start + SEL4])
                parts.append(level[at + SEL4:at + SEL3])
            s[base:base + 128] = jnp.concatenate(parts, 0).astype(s.dtype)
        for n in range(4):
            start = pl.multiple_of(64 * n + 16 * (y_pos ^ d), 16)
            s[256 + 16 * n:272 + 16 * n] = total[pl.ds(start, 16)].astype(s.dtype)


def reduce_z_kernel(pos, own, b1, b2, b3, s0, s1, s2, s3, total):
    z_pos = pos[2]
    total[...] = own[...] + b1[...].astype(F32) + b2[...].astype(F32) + b3[...].astype(F32)
    for d, s in enumerate((s0, s1, s2, s3)):
        s[0:SEL3] = total[SEL3 * d:SEL3 * d + SEL3].astype(s.dtype)
        s[SEL3:2 * SEL3] = total[128 + SEL3 * d:128 + SEL3 * d + SEL3].astype(s.dtype)
        start = pl.multiple_of(256 + 16 * (z_pos ^ d), 16)
        s[64:80] = total[pl.ds(start, 16)].astype(s.dtype)


def fold4_kernel(own, got, keep, send):
    keep[...] = own[...] + first_lanes(got[...], 3)
    send[...] = first_lanes(own[...], 1) + first_lanes(got[...], 2)


def mix_kernel(keep_a, keep_b, got, own, send):
    own[...] = keep_a[...] + got[0:T].astype(F32)
    send[...] = (keep_b[...] + got[T:2 * T].astype(F32)).astype(BF)


def natural_kernel(pos, e0, e1, dq_first, dk_a, dv_a, dq_a, dk_b, dv_b, dq_b, own2, got2, mix_own, mix_got, _s,
                   dq_out, dk_part, dv_part, dk_head, dv_head, mixed_out):
    mixed_out[...] = (mix_own[...] + mix_got[...].astype(F32)).astype(BF)
    level2 = own2[...] + got2[...].astype(F32)
    dq4 = e0[...] + e1[...]
    for p, (dk, dv, dq) in enumerate(((dk_a, dv_a, dq_a), (dk_b, dv_b, dq_b))):
        cols = slice(128 * p, 128 * p + 128)
        dk_top = dk[0:SEL2] + level2[0:SEL2, cols]
        dv_top = dv[0:SEL2] + level2[SEL2:2 * SEL2, cols]
        dk_head[:, cols] = dk_top[0:SEL3]
        dv_head[:, cols] = dv_top[0:SEL3]
        dq4_pair = jnp.concatenate([from_lanes(dq4, h, SEL4, 0.0) for h in (2 * p, 2 * p + 1)], 0)
        dq_t = jnp.concatenate([dq[:, 0:128] + dq_first[cols] + dq4_pair, dq[:, 128:T]], 1) * SCALE
        later = [
            jnp.concatenate([jnp.zeros((SEL3, 128), F32), top[SEL3:SEL2], rest[SEL2:T]], 0)
            for top, rest in ((dk_top, dk), (dv_top, dv))
        ]
        both = jnp.concatenate(later + [dq_t.T], 1).astype(BF)
        even = dot(put_mat(pos[0] * NH + 2 * p, T), both)
        odd = dot(put_mat(pos[0] * NH + 2 * p + 1, T), both)
        natural = jnp.where((iota(even.shape, 1) & 127) < HD, even, odd)
        dk_part[:, cols] = natural[:, 0:128].astype(BF)
        dv_part[:, cols] = natural[:, 128:256].astype(BF)
        dq_out[:, cols] = natural[:, 256:384].astype(BF)


def last_kernel(pos, own, b1, b2, b3, dk_head, dv_head, dk_part, dv_part, dk_out, dv_out, w_out):
    total = own[...] + b1[...].astype(F32) + b2[...].astype(F32) + b3[...].astype(F32)
    ks = (total[0:SEL3] + dk_head[...]).astype(BF)
    vs = (total[SEL3:2 * SEL3] + dv_head[...]).astype(BF)
    w_out[...] = total[64:80]
    mats = [put_mat(pos[0] * NH + m, SEL3) for m in range(NH)]
    ks, vs = per_head_rows(mats, [ks, vs])
    dk_out[...] = (ks + dk_part[...].astype(F32)).astype(BF)
    dv_out[...] = (vs + dv_part[...].astype(F32)).astype(BF)


def call(kernel, outs, *args, us=5, scratch=()):
    def spec(arg):
        return pl.BlockSpec(memory_space=pltpu.SMEM if arg.dtype == jnp.int32 else pltpu.VMEM)

    return pl.pallas_call(
        kernel,
        out_shape=[jax.ShapeDtypeStruct(shape, dtype) for shape, dtype in outs],
        in_specs=[spec(a) for a in args],
        out_specs=[pl.BlockSpec(memory_space=pltpu.VMEM)] * len(outs),
        scratch_shapes=scratch,
        compiler_params=pltpu.CompilerParams(vmem_limit_bytes=24 * 2 ** 20),
        cost_estimate=pl.CostEstimate(flops=us * 500_000_000, bytes_accessed=us * 1_000_000, transcendentals=0),
        name=getattr(kernel, "func", kernel).__name__,
    )(*args)


def swap_x(block, mask):
    return lax.ppermute(block, "seq", [(s, s ^ (16 * mask)) for s in range(64)])


def swap_z(block, mask):
    return lax.ppermute(block, "seq", [(s, s ^ (4 * mask)) for s in range(64)])


def swap_y(block, mask):
    return lax.ppermute(block, "seq", [(s, s ^ mask) for s in range(64)])


def swap(block, mask):
    return lax.ppermute(block, "head", [(s, s ^ mask) for s in range(4)])


def body(query_act, key_act, value_act, out_weight, cotangent):
    seq = lax.axis_index("seq")
    head = lax.axis_index("head")
    pos = jnp.stack([head, seq // 16, seq // 4 % 4, seq % 4]).astype(jnp.int32)
    wide, tall, stat = (T, F), (F, T), (8, T)

    (mine3,) = call(pick3_kernel, [((64, F), BF)], pos, key_act, value_act, us=1)
    pair_a = swap_z(mine3, 1)
    (mine2,) = call(pick2_kernel, [((256, F), BF)], pos, key_act, value_act, mine3, us=1)
    got2 = swap_y(mine2, 1)
    q, q_t, k, k_t, v, v_t, q4 = call(
        order_kernel, [(wide, BF), (tall, BF)] * 3 + [((16, F), BF)], pos, query_act, key_act, value_act, mine2, us=3,
    )
    (both,) = call(pair_kernel, [((128, F), BF)], mine3, pair_a, q, us=1)
    pair_b = swap_z(both, 3)
    (half2,) = call(pair_kernel, [((512, F), BF)], mine2, got2, both, us=1)
    kv2 = [half2, swap_y(half2, 3)]
    (q4_both,) = call(pair_kernel, [((32, F), BF)], q4, swap_x(q4, 1), both, us=1)
    q4 = [q4_both, swap_x(q4_both, 3)]
    pair_out = [(stat, F32), (stat, F32), ((128, T), F32)]
    m1a, l1a, o1a = call(functools.partial(first_kernel, 0), pair_out, q_t, k, v_t, half2, us=2)
    all3, cot = call(pack3_kernel, [((192, F), BF), (wide, BF)], pair_a, pair_b, cotangent, m1a, q4[1], us=1)
    kv3 = [*kv2, all3] + [swap_y(all3, n) for n in (1, 2, 3)]
    cot_z = swap(cot, 2)
    cot_c = swap(cot, 1)
    cot_zc = swap(cot_z, 1)
    cots = [cot, cot_c, cot_z, cot_zc]
    m1b, l1b, o1b = call(functools.partial(first_kernel, 1), pair_out, q_t, k, v_t, all3, us=2)
    m2, l2, o2 = call(
        second_kernel, [(stat, F32), (stat, F32), ((F, 128), F32)], *kv2, q, us=6
    )
    kv4, mine4 = call(part4_kernel, [((256, F), BF), ((HD + 8, 128), F32)], *kv3, *q4, m2, m1b, us=1)
    parts = [mine4] + [swap_x(mine4, n) for n in (1, 2, 3)]
    m, l, o, g, g_t, lse, delta, att_part = call(
        third_kernel,
        [((8, 128), F32), ((8, 128), F32), ((F, 128), F32), (wide, BF), (tall, BF), (stat, F32), (stat, F32),
         (tall, F32)],
        pos, *kv3, q, m1a, l1a, o1a, m1b, l1b, o1b, m2, l2, o2, *cots, out_weight, mine4, us=8,
    )
    lse, delta, att, *sent = call(
        fourth_kernel,
        [(stat, F32), (stat, F32), (tall, BF), ((272, F), F32)] + [((272, F), BF)] * 3,
        pos, *parts, m, l, o, g, g_t, lse, delta, att_part, *cots, us=6,
        scratch=[pltpu.VMEM((4, T, F), BF)],
    )
    own2, sent2, dq_first = call(
        second_back_kernel, [((512, F), F32), ((512, F), BF), ((F, 128), F32)],
        *kv2, q, g, lse, delta, us=2,
    )
    r4 = [sent[0]] + [swap_x(sent[n], n) for n in (1, 2, 3)]
    got2 = swap_y(sent2, 3)
    send_c, keep_a, keep_b = call(
        project_kernel, [((2 * T, F), BF), (wide, F32), (wide, F32)], pos, att, out_weight, sent2, us=2
    )
    dk3, dv3, dq_first, dk_a, dv_a, dq_a = call(
        third_back_kernel,
        [(wide, F32), (wide, F32), ((F, 128), F32), ((T, 128), F32), ((T, 128), F32), ((128, T), F32)],
        *kv3, q, q_t, k, k_t, v, g, g_t, lse, delta, dq_first, us=6,
    )
    own2, sent2 = call(fold_kernel, [((256, F), F32), ((256, F), BF)], own2, got2, r4[3], us=1)
    dk4, dv4, dq4 = call(
        fourth_back_kernel, [((128, F), F32), ((128, F), F32), ((HD, 128), F32)], kv4, *q4, *r4, us=1,
    )
    sent = call(
        reduce_y_kernel, [((320, F), F32)] + [((320, F), BF)] * 3, pos, *r4, dk4, dv4, dk3, dv3, sent2, us=1,
        scratch=[pltpu.VMEM((256, F), F32)],
    )
    got4 = swap_x(lax.optimization_barrier((dq4, sent[0]))[0], 3)
    dq4, dq4_send = call(fold4_kernel, [((HD, 128), F32)] * 2, dq4, got4, us=1)
    got4 = swap_x(dq4_send, 1)
    r3 = [sent[0]] + [swap_y(sent[n], n) for n in (1, 2, 3)]
    got_c = swap(lax.optimization_barrier((send_c, sent[0]))[0], 1)
    mix_own, mix_send = call(mix_kernel, [(wide, F32), (wide, BF)], keep_a, keep_b, got_c, us=1)
    mix_got = swap(mix_send, 2)
    got2 = swap_y(lax.optimization_barrier((sent2, r3[1]))[0], 1)
    dk_b, dv_b, dq_b = call(
        pair_back_kernel, [((T, 128), F32), ((T, 128), F32), ((128, T), F32)],
        q, q_t, k, k_t, v, g, g_t, lse, delta, sent[1], us=6,
    )
    sent = call(
        reduce_z_kernel, [((80, F), F32)] + [((80, F), BF)] * 3, pos, *r3, us=1,
        scratch=[pltpu.VMEM((320, F), F32)],
    )
    rz = [sent[0]] + [swap_z(sent[n], n) for n in (1, 2, 3)]
    query_grad, dk_part, dv_part, dk_head, dv_head, mixed_out = call(
        natural_kernel, [(wide, BF), (wide, BF), (wide, BF), ((SEL3, F), F32), ((SEL3, F), F32), (wide, BF)],
        pos, dq4, got4, dq_first, dk_a, dv_a, dq_a, dk_b, dv_b, dq_b, own2, got2, mix_own, mix_got, sent[1], us=6,
    )
    key_grad, value_grad, weight_grad = call(
        last_kernel, [(wide, BF), (wide, BF), ((16, F), F32)],
        pos, *rz, dk_head, dv_head, dk_part, dv_part, us=2,
    )
    return mixed_out, query_grad, key_grad, value_grad, weight_grad.T


def solution(mesh):
    rows = P("seq", "head")
    return jax.shard_map(
        body,
        mesh=mesh,
        in_specs=(rows, rows, rows, P("head", None), rows),
        out_specs=(rows, rows, rows, rows, P("head", "seq")),
        check_vma=False,
    )
```

```python
import functools

import functools

import jax
import jax.numpy as jnp
from jax import lax
from jax.experimental import pallas as pl
from jax.experimental.pallas import tpu as pltpu
from jax.sharding import PartitionSpec as P

HD = 64
NH = 4
T = 512
F = NH * HD
SEL2, SEL3, SEL4 = 128, 32, 8
SCALE = HD ** -0.5
NEG = -1e30
BF = jnp.bfloat16
F32 = jnp.float32


def iota(shape, dim):
    return lax.broadcasted_iota(jnp.int32, shape, dim)


def token_of(index):
    return (index >> 7) + ((index >> 5) & 3) * 4 + ((index >> 3) & 3) * 16 + (index & 7) * 64


def pick_mat(head, rows):
    wanted = (token_of(iota((rows, T), 0)) + head) & (T - 1)
    return jnp.where(wanted == iota((rows, T), 1), 1.0, 0.0).astype(BF)


def put_mat(head, cols):
    wanted = (token_of(iota((T, cols), 1)) + head) & (T - 1)
    return jnp.where(wanted == iota((T, cols), 0), 1.0, 0.0).astype(BF)


def dot(a, b, dims=((1,), (0,))):
    return lax.dot_general(a, b, (dims, ((), ())), preferred_element_type=F32)


def per_head_rows(mats, arrays):
    pairs = []
    for p in range(2):
        both = jnp.concatenate([a[:, 128 * p:128 * p + 128] for a in arrays], 1)
        even = dot(mats[2 * p], both)
        odd = dot(mats[2 * p + 1], both)
        pairs.append(jnp.where((iota(even.shape, 1) & 127) < HD, even, odd))
    return [
        jnp.concatenate([pair[:, 128 * n:128 * n + 128] for pair in pairs], 1)
        for n in range(len(arrays))
    ]


def head_blocks(rows, n):
    part = rows[:n]
    lane_head = iota(part.shape, 1) >> 6
    return jnp.concatenate([jnp.where(lane_head == h, part, 0.0) for h in range(NH)], 0)


def blocks_both(rows, n):
    full = head_blocks(rows, n)
    if NH * n < 128:
        full = jnp.concatenate([full, jnp.zeros((128 - NH * n, F), F32)], 0)
    return full.astype(BF), full.T.astype(BF)


def to_lanes(rows, n):
    total = None
    for h in range(NH):
        row = jnp.broadcast_to(jnp.where(iota((1, 128), 1) < n, rows[h], 0.0), (8, 128))
        if h:
            row = pltpu.roll(row, n * h, 1)
        total = row if total is None else total + row
    return total[0:1]


def from_lanes(rows, h, n, fill):
    if h:
        rows = pltpu.roll(rows, 128 - n * h, 1)
    return jnp.where(iota(rows.shape, 1) < n, rows, fill)


def soft(scores):
    peak = jnp.max(scores, axis=0, keepdims=True)
    weights = jnp.exp(scores - peak)
    return peak, jnp.sum(weights, axis=0, keepdims=True), weights.astype(BF)


def forward(keys, values, q_t):
    peak, total, weights = soft(dot(keys, q_t))
    return peak, total, dot(values, weights, ((0,), (0,)))


def backward(keys, values, q, q_t, g, g_t, lse, delta):
    prob = jnp.exp(dot(keys, q_t) - lse)
    ds = (prob * (dot(values, g_t) - delta)).astype(BF)
    d_values = dot(prob.astype(BF), g)
    d_keys = dot(ds, q)
    return d_keys, d_values, dot(keys, ds, ((0,), (0,)))


def diag_lanes(wide, n):
    return jnp.concatenate(
        [from_lanes(wide[HD * h:HD * h + HD], h, n, 0.0) for h in range(NH)], 0
    )


def half_mask(rows, h):
    return jnp.where((iota(rows.shape, 1) < HD) == (h % 2 == 0), rows.astype(F32), 0.0).astype(BF)


def half_pad(cols, h):
    zero = jnp.zeros_like(cols)
    return jnp.concatenate([cols, zero] if h % 2 == 0 else [zero, cols], 0)


def level1_backward(p, q_ref, q_t_ref, k_ref, k_t_ref, v_ref, g_ref, g_t_ref, lse_ref, delta_ref,
                    dk_ref, dv_ref, dq_ref):
    cols = slice(128 * p, 128 * p + 128)
    for h in (2 * p, 2 * p + 1):
        rows = slice(HD * h, HD * h + HD)
        for c in range(2):
            lanes = slice(256 * c, 256 * c + 256)
            q_t = half_pad(q_t_ref[rows, lanes], h)
            g_t = half_pad(g_t_ref[rows, lanes], h)
            prob = jnp.exp(dot(k_ref[:, cols], q_t) - lse_ref[h:h + 1, lanes])
            ds = (prob * (dot(v_ref[:, cols], g_t) - delta_ref[h:h + 1, lanes])).astype(BF)
            dv = dot(prob.astype(BF), half_mask(g_ref[lanes, cols], h))
            dk = dot(ds, half_mask(q_ref[lanes, cols], h))
            dq_ref[HD * (h % 2):HD * (h % 2) + HD, lanes] = dot(k_t_ref[rows, :], ds)
            if h % 2 == 0 and c == 0:
                dv_ref[...] = dv
                dk_ref[...] = dk
            else:
                dv_ref[...] += dv
                dk_ref[...] += dk


def blocks4(rows):
    full = jnp.concatenate([head_blocks(r.astype(F32), SEL4) for r in rows], 0)
    return full.astype(BF), full.T.astype(BF)


def fold_heads(wide):
    total = None
    for h in range(NH):
        part = wide[HD * h:HD * h + HD]
        part = jnp.where(((iota(part.shape, 1) >> 3) & 3) == h, part, 0.0)
        total = part if total is None else total + part
    return total


def first_lanes(rows, d):
    return pltpu.roll(rows, 128 - 32 * d, 1) if d else rows


def three(rows):
    high = rows.astype(BF)
    rest = rows - high.astype(F32)
    middle = rest.astype(BF)
    low = (rest - middle.astype(F32)).astype(BF)
    return [high.astype(F32), middle.astype(F32), low.astype(F32)]


def pick3_kernel(pos, k, v, out):
    mats = [pick_mat(pos[0] * NH + m, SEL3) for m in range(NH)]
    ks, vs = per_head_rows(mats, [k[...], v[...]])
    out[0:SEL3] = ks.astype(BF)
    out[SEL3:2 * SEL3] = vs.astype(BF)


def pick2_kernel(pos, k, v, _p3, out):
    mats = [pick_mat(pos[0] * NH + m, SEL2) for m in range(NH)]
    ks, vs = per_head_rows(mats, [k[...], v[...]])
    out[0:SEL2] = ks.astype(BF)
    out[SEL2:2 * SEL2] = vs.astype(BF)


def order_kernel(pos, q, k, v, _s, q_out, q_t_out, k_out, k_t_out, v_out, v_t_out, q4_out):
    mats = [pick_mat(pos[0] * NH + m, T) for m in range(NH)]
    qs, ks, vs = per_head_rows(mats, [q[...], k[...], v[...]])
    qs = qs * SCALE
    q_out[...] = qs.astype(BF)
    q4_out[...] = qs[0:16].astype(BF)
    q_t_out[...] = qs.T.astype(BF)
    k_out[...] = ks.astype(BF)
    k_t_out[...] = ks.T.astype(BF)
    v_out[...] = vs.astype(BF)
    v_t_out[...] = vs.T.astype(BF)


def first_kernel(p, q_t, k, v_t, _s, m_out, l_out, o_out):
    m_out[...] = jnp.zeros_like(m_out)
    l_out[...] = jnp.zeros_like(l_out)
    cols = slice(128 * p, 128 * p + 128)
    for h in range(2):
        rows_in = slice(HD * (2 * p + h), HD * (2 * p + h) + HD)
        rows = slice(HD * h, HD * h + HD)
        for c in range(2):
            lanes = slice(256 * c, 256 * c + 256)
            peak, total, weights = soft(dot(k[:, cols], half_pad(q_t[rows_in, lanes], h)))
            m_out[h:h + 1, lanes] = peak
            l_out[h:h + 1, lanes] = total
            o_out[rows, lanes] = dot(v_t[rows_in, :], weights)


def pair_kernel(a, b, _s, out):
    rows = a.shape[0]
    out[0:rows] = a[...]
    out[rows:2 * rows] = b[...]


def pack3_kernel(b, c, cot, _s, _t, out, cot_out):
    cot_out[...] = cot[...]
    for half in range(2):
        base = SEL3 * half
        for n, part in enumerate((b[base:base + SEL3], c[64 + base:64 + base + SEL3], c[base:base + SEL3])):
            out[96 * half + SEL3 * n:96 * half + SEL3 * n + SEL3] = part


def level2_places(a, b):
    return a.at[0:256], a.at[256:512], b.at[256:512], b.at[0:256]


def part4_kernel(a, b, c0, c1, c2, c3, qa, qb, _s, _t, out, part):
    for half in range(2):
        parts = []
        for here, others in zip(level2_places(a, b), (c0, c1, c2, c3)):
            parts.append(here[128 * half:128 * half + 16].astype(F32)[:SEL4])
            for n in range(3):
                start = 96 * half + SEL3 * n
                parts.append(others[start:start + 16].astype(F32)[:SEL4])
        out[128 * half:128 * half + 128] = jnp.concatenate(parts, 0).astype(BF)
    _, q_t = blocks4([qa[0:16], qa[16:32], qb[16:32], qb[0:16]])
    peak, total, weights = soft(dot(out[0:128], q_t))
    part[0:HD] = fold_heads(dot(out[128:256], weights, ((0,), (0,))))
    part[HD:HD + 8] = jnp.concatenate(
        [peak, total, jnp.zeros((6, 128), F32)], 0
    )


def stack_kv(refs):
    keys = jnp.concatenate([a[0:128] for a in refs], 0)
    values = jnp.concatenate([a[128:256] for a in refs], 0)
    return keys, values


def stack_kv3(a, b, others):
    keys, values = [], []
    for here, other in zip(level2_places(a, b), others):
        keys += [here[0:SEL3], other[0:96]]
        values += [here[128:128 + SEL3], other[96:192]]
    return jnp.concatenate(keys, 0), jnp.concatenate(values, 0)


def second_kernel(a, b, q, m_out, l_out, o_out):
    keys, values = stack_kv((a.at[0:256], a.at[256:512], b.at[0:256], b.at[256:512]))
    _, q_t = blocks_both(q[0:SEL2].astype(F32), SEL2)
    peak, total, wide = forward(keys, values, q_t)
    m_out[...] = jnp.broadcast_to(peak, m_out.shape)
    l_out[...] = jnp.broadcast_to(total, l_out.shape)
    o_out[...] = jnp.concatenate(
        [wide[HD * h:HD * h + HD, 128 * h:128 * h + 128] for h in range(NH)], 0
    )


def third_kernel(pos, a, b, a0, a1, a2, a3, q, m1a, l1a, o1a, m1b, l1b, o1b, m2, l2, o2, c0, c1, c2, c3, w, _p3,
                 m_out, l_out, o_out, g_out, g_t_out, lse_out, delta_out, att_out):
    here = pos[0]
    grad = None
    for r, c in enumerate((c0, c1, c2, c3)):
        at = pl.multiple_of((here ^ r) * F, F)
        term = dot(c[...], w[:, pl.ds(at, F)], ((1,), (1,)))
        grad = term if grad is None else grad + term
    mats = [pick_mat(here * NH + m, T) for m in range(NH)]
    (gs,) = per_head_rows(mats, [grad.astype(BF)])
    g_t = gs.T
    g_out[...] = gs.astype(BF)
    g_t_out[...] = g_t.astype(BF)

    keys, values = stack_kv3(a, b, (a0, a1, a2, a3))
    _, q_t = blocks_both(q[0:SEL3].astype(F32), SEL3)
    m3, l3, wide = forward(keys, values, q_t)
    m3 = jnp.broadcast_to(m3, (8, 128))
    l3 = jnp.broadcast_to(l3, (8, 128))
    lse_out[...] = jnp.zeros_like(lse_out)
    delta_out[...] = jnp.zeros_like(delta_out)
    m_out[...] = jnp.zeros_like(m_out)
    l_out[...] = jnp.zeros_like(l_out)
    for h in range(NH):
        rows = slice(HD * h, HD * h + HD)
        m1, l1, o1 = ((m1a, l1a, o1a), (m1b, l1b, o1b))[h // 2]
        one, half = slice(h % 2, h % 2 + 1), slice(HD * (h % 2), HD * (h % 2) + HD)
        ma, la, oa = m1[one, 0:128], l1[one, 0:128], o1[half, 0:128]
        mb, lb = m2[0:1, 128 * h:128 * h + 128], l2[0:1, 128 * h:128 * h + 128]
        mc = from_lanes(m3, h, SEL3, NEG)[0:1]
        lc = from_lanes(l3, h, SEL3, 0.0)[0:1]
        oc = from_lanes(wide[rows], h, SEL3, 0.0)
        top = jnp.maximum(jnp.maximum(ma, mb), mc)
        fa, fb, fc = jnp.exp(ma - top), jnp.exp(mb - top), jnp.exp(mc - top)
        m_out[h:h + 1] = top
        l_out[h:h + 1] = fa * la + fb * lb + fc * lc
        o_out[rows] = fa * oa + fb * o2[rows] + fc * oc
        total = l1[one, 128:T]
        out = o1[half, 128:T] / total
        lse_out[h:h + 1, 128:T] = m1[one, 128:T] + jnp.log(total)
        delta_out[h:h + 1, 128:T] = jnp.sum(g_t_out[rows, 128:T].astype(F32) * out, axis=0, keepdims=True)
        att_out[rows] = dot(out.astype(BF), mats[h][128:T])


def fourth_kernel(pos, r0, r1, r2, r3, m, l, o, g, g_t, lse_in, delta_in, att_in, c0, c1, c2, c3,
                  lse_out, delta_out, att_out, s0, s1, s2, s3, blocks):
    here, x_pos = pos[0], pos[1]
    parts = [first_lanes(r[...], d) for d, r in enumerate((r0, r1, r2, r3))]
    peaks = [r[HD:HD + 8] for r in parts]
    peak = jnp.maximum(jnp.maximum(peaks[0], peaks[1]), jnp.maximum(peaks[2], peaks[3]))[0:1]
    total, weighted = 0.0, 0.0
    for r in parts:
        factor = jnp.exp(r[HD:HD + 1] - peak)
        total = total + factor * r[HD + 1:HD + 2]
        weighted = weighted + factor * r[0:HD]
    peak = jnp.broadcast_to(peak, (8, 128))
    total = jnp.broadcast_to(total, (8, 128))
    lse_out[...] = lse_in[...]
    delta_out[...] = delta_in[...]
    lse_rows, delta_rows = [], []
    for h in range(NH):
        rows = slice(HD * h, HD * h + HD)
        ma, la, oa = m[h:h + 1], l[h:h + 1], o[rows]
        mb = from_lanes(peak, h, SEL4, NEG)[0:1]
        lb = from_lanes(total, h, SEL4, 0.0)[0:1]
        ob = from_lanes(weighted, h, SEL4, 0.0)
        top = jnp.maximum(ma, mb)
        fa, fb = jnp.exp(ma - top), jnp.exp(mb - top)
        denominator = fa * la + fb * lb
        out = (fa * oa + fb * ob) / denominator
        lse = top + jnp.log(denominator)
        delta = jnp.sum(g_t[rows, 0:128].astype(F32) * out, axis=0, keepdims=True)
        lse_out[h:h + 1, 0:128] = lse
        delta_out[h:h + 1, 0:128] = delta
        lse_rows.append(lse)
        delta_rows.append(delta)
        att = att_in[rows] + dot(out.astype(BF), pick_mat(here * NH + h, SEL2))
        att_out[rows] = att.astype(BF)
    stats = three(to_lanes(lse_rows, SEL4)) + three(to_lanes(delta_rows, SEL4)) + [jnp.zeros((2, 128), F32)]
    stats = jnp.concatenate(stats, 0)
    stats = jnp.concatenate([g[0:16].astype(F32)[0:SEL4], jnp.concatenate([stats, stats], 1)], 0).astype(BF)
    for r, c in enumerate((c0, c1, c2, c3)):
        blocks[here ^ r] = c[...]
    for d, s in enumerate((s0, s1, s2, s3)):
        term = dot(att_out[...], blocks[x_pos ^ d])
        s[0:256] = term.T.astype(s.dtype)
        s[256:272] = stats.astype(s.dtype)


def fourth_back_kernel(kv, qa, qb, b0, b1, b2, b3, d_keys, d_values, dq):
    q, q_t = blocks4([qa[0:16], qa[16:32], qb[16:32], qb[0:16]])
    news = [b[256:272].astype(F32) for b in (b0, b1, b2, b3)]
    g, g_t = blocks4(news)
    lse, delta = 0.0, 0.0
    for d, new in enumerate(news):
        for start in range(3):
            row_l = jnp.where(iota((1, 128), 1) < 32, new[8 + start:9 + start, 0:128], 0.0)
            row_d = jnp.where(iota((1, 128), 1) < 32, new[11 + start:12 + start, 0:128], 0.0)
            both = jnp.concatenate([row_l, row_d, jnp.zeros((6, 128), F32)], 0)
            both = pltpu.roll(both, 32 * d, 1) if d else both
            lse = lse + both[0:1]
            delta = delta + both[1:2]
    d_keys[...], d_values[...], wide = backward(kv[0:128], kv[128:256], q, q_t, g, g_t, lse, delta)
    dq[...] = fold_heads(wide)


def project_kernel(pos, att, w, _s, send, keep_a, keep_b):
    here = pos[0]
    for r, ref in ((0, keep_a), (2, keep_b), (1, send.at[0:T]), (3, send.at[T:2 * T])):
        at = pl.multiple_of((here ^ r) * F, F)
        ref[...] = dot(att[...], w[:, pl.ds(at, F)], ((0,), (0,))).astype(ref.dtype)


def second_back_kernel(a, b, q, g, lse, delta, own, send, dq_first):
    keys, values = stack_kv((a.at[0:256], a.at[256:512], b.at[0:256], b.at[256:512]))
    q2, q2_t = blocks_both(q[0:SEL2].astype(F32), SEL2)
    g2, g2_t = blocks_both(g[0:SEL2].astype(F32), SEL2)
    lse2 = jnp.concatenate([lse[h:h + 1, 0:128] for h in range(NH)], 1)
    delta2 = jnp.concatenate([delta[h:h + 1, 0:128] for h in range(NH)], 1)
    d_keys, d_values, wide = backward(keys, values, q2, q2_t, g2, g2_t, lse2, delta2)
    diag = [wide[HD * h:HD * h + HD, 128 * h:128 * h + 128] for h in range(NH)]
    dq_first[...] = jnp.concatenate(diag, 0)
    for n, (out, at) in enumerate(((own, 0), (own, 256), (send, 0), (send, 256))):
        out[at:at + 128] = d_keys[128 * n:128 * n + 128].astype(out.dtype)
        out[at + 128:at + 256] = d_values[128 * n:128 * n + 128].astype(out.dtype)


def fold_kernel(own, got, _s, keep, send):
    keep[...] = own[0:256] + got[0:256].astype(F32)
    send[...] = (own[256:512] + got[256:512].astype(F32)).astype(BF)


def third_back_kernel(a, b, a0, a1, a2, a3, q, q_t, k, k_t, v, g, g_t, lse, delta, dq_in,
                      dk3, dv3, dq_first, dk, dv, dq):
    keys, values = stack_kv3(a, b, (a0, a1, a2, a3))
    q3, q3_t = blocks_both(q[0:SEL3].astype(F32), SEL3)
    g3, g3_t = blocks_both(g[0:SEL3].astype(F32), SEL3)
    lse3 = to_lanes([lse[h:h + 1, 0:128] for h in range(NH)], SEL3)
    delta3 = to_lanes([delta[h:h + 1, 0:128] for h in range(NH)], SEL3)
    dk3[...], dv3[...], wide = backward(keys, values, q3, q3_t, g3, g3_t, lse3, delta3)
    dq_first[...] = dq_in[...] + diag_lanes(wide, SEL3)
    level1_backward(0, q, q_t, k, k_t, v, g, g_t, lse, delta, dk, dv, dq)


def pair_back_kernel(q, q_t, k, k_t, v, g, g_t, lse, delta, _s, dk, dv, dq):
    level1_backward(1, q, q_t, k, k_t, v, g, g_t, lse, delta, dk, dv, dq)


def reduce_y_kernel(pos, own, b1, b2, b3, dk4, dv4, dk3, dv3, _s, s0, s1, s2, s3, total):
    y_pos = pos[3]
    total[...] = own[0:256] + b1[0:256].astype(F32) + b2[0:256].astype(F32) + b3[0:256].astype(F32)
    for d, s in enumerate((s0, s1, s2, s3)):
        for base, level, fourth in ((0, dk3, dk4), (128, dv3, dv4)):
            parts = []
            for n in range(4):
                at = 128 * d + SEL3 * n
                start = SEL3 * d + SEL4 * n
                parts.append(level[at:at + SEL4] + fourth[start:start + SEL4])
                parts.append(level[at + SEL4:at + SEL3])
            s[base:base + 128] = jnp.concatenate(parts, 0).astype(s.dtype)
        for n in range(4):
            start = pl.multiple_of(64 * n + 16 * (y_pos ^ d), 16)
            s[256 + 16 * n:272 + 16 * n] = total[pl.ds(start, 16)].astype(s.dtype)


def reduce_z_kernel(pos, own, b1, b2, b3, s0, s1, s2, s3, total):
    z_pos = pos[2]
    total[...] = own[...] + b1[...].astype(F32) + b2[...].astype(F32) + b3[...].astype(F32)
    for d, s in enumerate((s0, s1, s2, s3)):
        s[0:SEL3] = total[SEL3 * d:SEL3 * d + SEL3].astype(s.dtype)
        s[SEL3:2 * SEL3] = total[128 + SEL3 * d:128 + SEL3 * d + SEL3].astype(s.dtype)
        start = pl.multiple_of(256 + 16 * (z_pos ^ d), 16)
        s[64:80] = total[pl.ds(start, 16)].astype(s.dtype)


def fold4_kernel(own, got, keep, send):
    keep[...] = own[...] + first_lanes(got[...], 3)
    send[...] = first_lanes(own[...], 1) + first_lanes(got[...], 2)


def mix_kernel(keep_a, keep_b, got, own, send):
    own[...] = keep_a[...] + got[0:T].astype(F32)
    send[...] = (keep_b[...] + got[T:2 * T].astype(F32)).astype(BF)


def natural_kernel(pos, e0, e1, dq_first, dk_a, dv_a, dq_a, dk_b, dv_b, dq_b, own2, got2, mix_own, mix_got, _s,
                   dq_out, dk_part, dv_part, dk_head, dv_head, mixed_out):
    mixed_out[...] = (mix_own[...] + mix_got[...].astype(F32)).astype(BF)
    level2 = own2[...] + got2[...].astype(F32)
    dq4 = e0[...] + e1[...]
    for p, (dk, dv, dq) in enumerate(((dk_a, dv_a, dq_a), (dk_b, dv_b, dq_b))):
        cols = slice(128 * p, 128 * p + 128)
        dk_top = dk[0:SEL2] + level2[0:SEL2, cols]
        dv_top = dv[0:SEL2] + level2[SEL2:2 * SEL2, cols]
        dk_head[:, cols] = dk_top[0:SEL3]
        dv_head[:, cols] = dv_top[0:SEL3]
        dq4_pair = jnp.concatenate([from_lanes(dq4, h, SEL4, 0.0) for h in (2 * p, 2 * p + 1)], 0)
        dq_t = jnp.concatenate([dq[:, 0:128] + dq_first[cols] + dq4_pair, dq[:, 128:T]], 1) * SCALE
        later = [
            jnp.concatenate([jnp.zeros((SEL3, 128), F32), top[SEL3:SEL2], rest[SEL2:T]], 0)
            for top, rest in ((dk_top, dk), (dv_top, dv))
        ]
        both = jnp.concatenate(later + [dq_t.T], 1).astype(BF)
        even = dot(put_mat(pos[0] * NH + 2 * p, T), both)
        odd = dot(put_mat(pos[0] * NH + 2 * p + 1, T), both)
        natural = jnp.where((iota(even.shape, 1) & 127) < HD, even, odd)
        dk_part[:, cols] = natural[:, 0:128].astype(BF)
        dv_part[:, cols] = natural[:, 128:256].astype(BF)
        dq_out[:, cols] = natural[:, 256:384].astype(BF)


def last_kernel(pos, own, b1, b2, b3, dk_head, dv_head, dk_part, dv_part, dk_out, dv_out, w_out):
    total = own[...] + b1[...].astype(F32) + b2[...].astype(F32) + b3[...].astype(F32)
    ks = (total[0:SEL3] + dk_head[...]).astype(BF)
    vs = (total[SEL3:2 * SEL3] + dv_head[...]).astype(BF)
    w_out[...] = total[64:80]
    mats = [put_mat(pos[0] * NH + m, SEL3) for m in range(NH)]
    ks, vs = per_head_rows(mats, [ks, vs])
    dk_out[...] = (ks + dk_part[...].astype(F32)).astype(BF)
    dv_out[...] = (vs + dv_part[...].astype(F32)).astype(BF)


def call(kernel, outs, *args, us=5, scratch=()):
    def spec(arg):
        return pl.BlockSpec(memory_space=pltpu.SMEM if arg.dtype == jnp.int32 else pltpu.VMEM)

    return pl.pallas_call(
        kernel,
        out_shape=[jax.ShapeDtypeStruct(shape, dtype) for shape, dtype in outs],
        in_specs=[spec(a) for a in args],
        out_specs=[pl.BlockSpec(memory_space=pltpu.VMEM)] * len(outs),
        scratch_shapes=scratch,
        compiler_params=pltpu.CompilerParams(vmem_limit_bytes=24 * 2 ** 20),
        cost_estimate=pl.CostEstimate(flops=us * 500_000_000, bytes_accessed=us * 1_000_000, transcendentals=0),
        name=getattr(kernel, "func", kernel).__name__,
    )(*args)


def swap_x(block, mask):
    return lax.ppermute(block, "seq", [(s, s ^ (16 * mask)) for s in range(64)])


def swap_z(block, mask):
    return lax.ppermute(block, "seq", [(s, s ^ (4 * mask)) for s in range(64)])


def swap_y(block, mask):
    return lax.ppermute(block, "seq", [(s, s ^ mask) for s in range(64)])


def swap(block, mask):
    return lax.ppermute(block, "head", [(s, s ^ mask) for s in range(4)])


def body(query_act, key_act, value_act, out_weight, cotangent):
    seq = lax.axis_index("seq")
    head = lax.axis_index("head")
    pos = jnp.stack([head, seq // 16, seq // 4 % 4, seq % 4]).astype(jnp.int32)
    wide, tall, stat = (T, F), (F, T), (8, T)

    (mine3,) = call(pick3_kernel, [((64, F), BF)], pos, key_act, value_act, us=1)
    pair_a = swap_z(mine3, 1)
    (mine2,) = call(pick2_kernel, [((256, F), BF)], pos, key_act, value_act, mine3, us=1)
    got2 = swap_y(mine2, 1)
    q, q_t, k, k_t, v, v_t, q4 = call(
        order_kernel, [(wide, BF), (tall, BF)] * 3 + [((16, F), BF)], pos, query_act, key_act, value_act, mine2, us=3,
    )
    (both,) = call(pair_kernel, [((128, F), BF)], mine3, pair_a, q, us=1)
    pair_b = swap_z(both, 3)
    (half2,) = call(pair_kernel, [((512, F), BF)], mine2, got2, both, us=1)
    kv2 = [half2, swap_y(half2, 3)]
    (q4_both,) = call(pair_kernel, [((32, F), BF)], q4, swap_x(q4, 1), both, us=1)
    q4 = [q4_both, swap_x(q4_both, 3)]
    pair_out = [(stat, F32), (stat, F32), ((128, T), F32)]
    m1a, l1a, o1a = call(functools.partial(first_kernel, 0), pair_out, q_t, k, v_t, half2, us=2)
    all3, cot = call(pack3_kernel, [((192, F), BF), (wide, BF)], pair_a, pair_b, cotangent, m1a, q4[1], us=1)
    kv3 = [*kv2, all3] + [swap_y(all3, n) for n in (1, 2, 3)]
    cot_z = swap(cot, 2)
    cot_c = swap(cot, 1)
    cot_zc = swap(cot_z, 1)
    cots = [cot, cot_c, cot_z, cot_zc]
    m1b, l1b, o1b = call(functools.partial(first_kernel, 1), pair_out, q_t, k, v_t, all3, us=2)
    m2, l2, o2 = call(
        second_kernel, [(stat, F32), (stat, F32), ((F, 128), F32)], *kv2, q, us=6
    )
    kv4, mine4 = call(part4_kernel, [((256, F), BF), ((HD + 8, 128), F32)], *kv3, *q4, m2, m1b, us=1)
    parts = [mine4] + [swap_x(mine4, n) for n in (1, 2, 3)]
    m, l, o, g, g_t, lse, delta, att_part = call(
        third_kernel,
        [((8, 128), F32), ((8, 128), F32), ((F, 128), F32), (wide, BF), (tall, BF), (stat, F32), (stat, F32),
         (tall, F32)],
        pos, *kv3, q, m1a, l1a, o1a, m1b, l1b, o1b, m2, l2, o2, *cots, out_weight, mine4, us=8,
    )
    lse, delta, att, *sent = call(
        fourth_kernel,
        [(stat, F32), (stat, F32), (tall, BF), ((272, F), F32)] + [((272, F), BF)] * 3,
        pos, *parts, m, l, o, g, g_t, lse, delta, att_part, *cots, us=6,
        scratch=[pltpu.VMEM((4, T, F), BF)],
    )
    own2, sent2, dq_first = call(
        second_back_kernel, [((512, F), F32), ((512, F), BF), ((F, 128), F32)],
        *kv2, q, g, lse, delta, us=2,
    )
    r4 = [sent[0]] + [swap_x(sent[n], n) for n in (1, 2, 3)]
    got2 = swap_y(sent2, 3)
    send_c, keep_a, keep_b = call(
        project_kernel, [((2 * T, F), BF), (wide, F32), (wide, F32)], pos, att, out_weight, sent2, us=2
    )
    dk3, dv3, dq_first, dk_a, dv_a, dq_a = call(
        third_back_kernel,
        [(wide, F32), (wide, F32), ((F, 128), F32), ((T, 128), F32), ((T, 128), F32), ((128, T), F32)],
        *kv3, q, q_t, k, k_t, v, g, g_t, lse, delta, dq_first, us=6,
    )
    own2, sent2 = call(fold_kernel, [((256, F), F32), ((256, F), BF)], own2, got2, r4[3], us=1)
    dk4, dv4, dq4 = call(
        fourth_back_kernel, [((128, F), F32), ((128, F), F32), ((HD, 128), F32)], kv4, *q4, *r4, us=1,
    )
    sent = call(
        reduce_y_kernel, [((320, F), F32)] + [((320, F), BF)] * 3, pos, *r4, dk4, dv4, dk3, dv3, sent2, us=1,
        scratch=[pltpu.VMEM((256, F), F32)],
    )
    got4 = swap_x(lax.optimization_barrier((dq4, sent[0]))[0], 3)
    dq4, dq4_send = call(fold4_kernel, [((HD, 128), F32)] * 2, dq4, got4, us=1)
    got4 = swap_x(dq4_send, 1)
    r3 = [sent[0]] + [swap_y(sent[n], n) for n in (1, 2, 3)]
    got_c = swap(lax.optimization_barrier((send_c, sent[0]))[0], 1)
    mix_own, mix_send = call(mix_kernel, [(wide, F32), (wide, BF)], keep_a, keep_b, got_c, us=1)
    mix_got = swap(mix_send, 2)
    dk_b, dv_b, dq_b = call(
        pair_back_kernel, [((T, 128), F32), ((T, 128), F32), ((128, T), F32)],
        q, q_t, k, k_t, v, g, g_t, lse, delta, sent[1], us=6,
    )
    got2 = swap_y(lax.optimization_barrier((sent2, r3[1], dk_b))[0], 1)
    sent = call(
        reduce_z_kernel, [((80, F), F32)] + [((80, F), BF)] * 3, pos, *r3, us=1,
        scratch=[pltpu.VMEM((320, F), F32)],
    )
    rz = [sent[0]] + [swap_z(sent[n], n) for n in (1, 2, 3)]
    query_grad, dk_part, dv_part, dk_head, dv_head, mixed_out = call(
        natural_kernel, [(wide, BF), (wide, BF), (wide, BF), ((SEL3, F), F32), ((SEL3, F), F32), (wide, BF)],
        pos, dq4, got4, dq_first, dk_a, dv_a, dq_a, dk_b, dv_b, dq_b, own2, got2, mix_own, mix_got, sent[1], us=6,
    )
    key_grad, value_grad, weight_grad = call(
        last_kernel, [(wide, BF), (wide, BF), ((16, F), F32)],
        pos, *rz, dk_head, dv_head, dk_part, dv_part, us=2,
    )
    return mixed_out, query_grad, key_grad, value_grad, weight_grad.T


def solution(mesh):
    rows = P("seq", "head")
    return jax.shard_map(
        body,
        mesh=mesh,
        in_specs=(rows, rows, rows, P("head", None), rows),
        out_specs=(rows, rows, rows, rows, P("head", "seq")),
        check_vma=False,
    )
```
